32 devices in a mesh: lat: 4 (over z), lon: 8 (over y, x, core).
Axes of the slice: x: 2, y: 2, z: 4, core: 2. Of those that a mesh axis runs over, the one named last changes fastest.
Arguments:
- features: bfloat16 [16384, 64], P(('lat', 'lon')), may hold values from -6 to 6
- land_tile: int32 [16384, 1], P(('lat', 'lon')), may hold values from 0 to 31; in each aligned block of 512 rows (0 to 511, 512 to 1023, ...) at most 32 rows name the same one
- land_spot: int32 [16384], P(('lat', 'lon')), may hold values from 0 to 1023
- w_in: bfloat16 [64, 256], replicated, may hold values from -0.75 to 0.75
- b_in: float32 [256], replicated, may hold values from -3 to 3
- w_mid: bfloat16 [256, 256], replicated, may hold values from -0.375 to 0.375
- b_mid: float32 [256], replicated, may hold values from -3 to 3
- w_out: bfloat16 [256, 16], replicated, may hold values from -0.375 to 0.375
- tracers: float32 [16, 16, 32, 1024], P(None, None, 'lat', 'lon'), may hold values from -6 to 6
- zonal_wind: float32 [16, 32, 1024], P(None, 'lat', 'lon'), may hold values from -0.95 to 0.95
- meridional_wind: float32 [16, 32, 1024], P(None, 'lat', 'lon'), may hold values from -0.95 to 0.95
- mixing: float32 [32, 16, 16], P('lat'), may hold values from 0 to 0.8, as said below
Outputs:
- tracers_out: float32 [16, 16, 32, 1024], P(None, None, 'lat', 'lon')
The draws below stay inside these ranges and needn't reach their ends.
Inputs may be any that keep to these rules, and one draw needn't show every extreme that they name: `land_tile`: in each aligned block of 512 rows (the land cells of one device), no tile is named by more than 32 rows, a bound that some block reaches; every tile is named somewhere. `mixing`: entries are nonnegative.
All inputs are finite; a program needn't handle non-finite values.
Results may differ from the reference program's by a relative error of at most 0.00044.
Values sent between devices are 32-bit elements; how exact they have to be, the bound alone decides.
A program may use at most 64 MiB of HBM per device.

```python
import math
import jax
import jax.numpy as jnp
import numpy as np
from jax import lax

TR = 16
LEV = 16
FEAT = 64
HID = 256
SUBSTEPS = 2
LAND_DEV = 512
CLAT = 8
CLON = 128
CAP = 32
LAND = 16384
NLAT = 32
NLON = 1024
N_LON = 8
DEVICES = 32


def draw_mixing(key, part):
    key_diag = jax.random.fold_in(key, 11)
    key_off = jax.random.fold_in(key, 12)
    diag_part = jax.random.uniform(key_diag, (NLAT, LEV), jnp.float32, 0.5, 0.8)
    off_part = jax.random.uniform(key_off, (NLAT, LEV, LEV), jnp.float32, 0.0, 1.0) * (0.5 / LEV)
    identity = jnp.eye(LEV, dtype=jnp.float32)
    return off_part * (1.0 - identity)[None] + diag_part[:, :, None] * identity[None]


def touch_ends(array, rng, low, top_value):
    extent = array.shape
    place = [jax.random.randint(jax.random.fold_in(rng, axis), (), 0, extent[axis]) for axis in range(len(extent))]
    array = array.at[tuple(place)].set(low)
    longest = extent.index(max(extent))
    place[longest] = (place[longest] + 1) % extent[longest]
    return array.at[tuple(place)].set(top_value)


def level_of(key, extent, cuts, low, largest):
    def one(dim, shards_of):
        steps = jax.random.uniform(jax.random.fold_in(jax.random.fold_in(key, 6), dim), (shards_of,), jnp.float32, low / len(cuts), largest / len(cuts))
        return jnp.repeat(jnp.exp(steps), extent[dim] // shards_of).reshape((-1,) + (1,) * (len(extent) - dim - 1))

    level = one(*cuts[0])
    for cut in cuts[1:]:
        level = level * one(*cut)
    return level


def shared_out(stream_key, own, number, rows, number_of, top, limit, lean):
    ranking = jax.random.permutation(stream_key, number_of)
    crowded, usual = shares(number_of, rows * top, limit, lean, True), shares(number_of, rows * top, limit, lean, False)
    places = jnp.arange(number_of)

    def named(tallies, offset_by):
        used = int((tallies > 0).sum())
        fixed = max(1, used // 4)
        shifted = fixed + (places - fixed + offset_by * (used - fixed)) % max(1, number_of - fixed)
        return jnp.zeros((number_of,), jnp.int32).at[ranking[jnp.where(places < fixed, places, shifted)]].set(jnp.asarray(tallies, jnp.int32))

    tallies = jnp.where(number % 4 == 0, named(crowded, number // 4), named(usual, number - number // 4 - 1))
    mixed = jax.random.permutation(jax.random.fold_in(own, 3), number_of)
    source_of, sink = mixed[0:number_of // 2 * 2:2], mixed[1:number_of // 2 * 2:2]
    margin = jnp.minimum(tallies[source_of] - 1, limit - tallies[sink]) // 2
    margin = jnp.where((source_of == ranking[0]) | (sink == ranking[0]) | (tallies[sink] == 0), 0, jnp.maximum(margin, 0))
    shifted = jax.random.randint(jax.random.fold_in(own, 4), (number_of // 2,), 0, 1 << 20) % (margin + 1)
    tallies = tallies.at[source_of].add(-shifted).at[sink].add(shifted)
    labels = jnp.searchsorted(jnp.cumsum(tallies), jnp.arange(rows * top), side="right").astype(jnp.int32)
    grid = labels.reshape(top, rows).T
    grid = grid[jax.random.permutation(jax.random.fold_in(own, 1), rows)]
    offset_by = jax.random.randint(jax.random.fold_in(own, 2), (rows, 1), 0, top)
    return jnp.take_along_axis(grid, (jnp.arange(top)[None, :] + offset_by) % top, axis=1)


def shares(number_of, total, limit, skew, full):
    weights = [(1 << 20) // math.isqrt(grade ** skew) + 1 for grade in range(1, number_of + 1)]
    largest = limit if full else min(limit, max(-(-total // number_of), total * weights[0] // sum(weights)))
    least = 1 if total - largest >= number_of - 1 else 0
    holding, surplus = [largest] + [least] * (number_of - 1), total - largest - least * (number_of - 1)
    while surplus > 0:
        free = [i for i in range(1, number_of) if holding[i] < largest] or [i for i in range(1, number_of) if holding[i] < limit]
        whole, remaining = sum([weights[i] for i in free]), surplus
        for i in free:
            more = min(limit - holding[i], max(1, remaining * weights[i] // whole), surplus)
            holding[i] = holding[i] + more
            surplus = surplus - more
    return np.array(holding)


def centred(rng, dims, spread, most, shards=(), kind=jnp.bfloat16):
    result = spread * jax.random.normal(rng, dims, jnp.float32)
    if shards:
        result = result * level_of(rng, dims, shards, -0.22, 0.18)
    return jnp.clip(result, -most, most).astype(kind)


def setup_inputs(seed: int = 0) -> dict:
    key_of = jax.random.split(jax.random.key(seed), 13)
    features = centred(key_of[0], (LAND, FEAT), 1.0, 6.0, ((0, 32),))
    land_tile_keys = jax.random.split(jax.random.fold_in(key_of[1], 1), LAND // LAND_DEV)
    land_tile_turns = jax.random.permutation(jax.random.fold_in(key_of[1], 3), LAND // LAND_DEV)
    land_tile = jax.vmap(lambda own, number: shared_out(jax.random.fold_in(key_of[1], 2), own, number, LAND_DEV, DEVICES, 1, CAP, 2))(land_tile_keys, land_tile_turns).reshape((LAND, 1))
    land_spot = touch_ends(jax.random.randint(key_of[2], (LAND,), 0, CLAT * CLON), jax.random.fold_in(key_of[2], 1), 0, (CLAT * CLON) - 1).astype(jnp.int32)
    w_in = centred(key_of[3], (FEAT, HID), FEAT ** -0.5, 0.75)
    b_in = centred(key_of[4], (HID,), 0.5, 3.0, (), jnp.float32)
    w_mid = centred(key_of[5], (HID, HID), HID ** -0.5, 0.375)
    b_mid = centred(key_of[6], (HID,), 0.5, 3.0, (), jnp.float32)
    w_out = centred(key_of[7], (HID, TR), HID ** -0.5, 0.375)
    tracers = centred(key_of[8], (TR, LEV, NLAT, NLON), 1.0, 6.0, ((2, 4), (3, 8)), jnp.float32)
    zonal_wind = jnp.clip(jax.random.uniform(key_of[9], (LEV, NLAT, NLON), jnp.float32, -0.95, 0.95) * level_of(key_of[9], (LEV, NLAT, NLON), ((1, 4), (2, 8)), -0.4, 0.0), -0.95, 0.95)
    meridional_wind = jnp.clip(jax.random.uniform(key_of[10], (LEV, NLAT, NLON), jnp.float32, -0.95, 0.95) * level_of(key_of[10], (LEV, NLAT, NLON), ((1, 4), (2, 8)), -0.4, 0.0), -0.95, 0.95)
    mixing = draw_mixing(jax.random.fold_in(key_of[12], 71), 0)
    return dict(features=features, land_tile=land_tile, land_spot=land_spot, w_in=w_in, b_in=b_in, w_mid=w_mid, b_mid=b_mid, w_out=w_out, tracers=tracers, zonal_wind=zonal_wind, meridional_wind=meridional_wind, mixing=mixing)


def section(values, start, stop, axis):
    return lax.slice_in_dim(values, start, values.shape[axis] + stop, axis=axis)


def transport(values, courant, axis):
    edges = 7.0 / 12.0 * (section(values, 1, -2, axis) + section(values, 2, -1, axis)) - 1.0 / 12.0 * (section(values, 0, -3, axis) + section(values, 3, 0, axis))
    left_edge = section(edges, 0, -1, axis)
    right_edge = section(edges, 1, 0, axis)
    centre = section(values, 2, -2, axis)
    slope = right_edge - left_edge
    curve = 6.0 * (centre - 0.5 * (left_edge + right_edge))
    face_courant = section(courant, 2, -3, axis)
    upwind = face_courant * (section(right_edge, 0, -1, axis) - 0.5 * face_courant * (section(slope, 0, -1, axis) - (1.0 - 2.0 / 3.0 * face_courant) * section(curve, 0, -1, axis)))
    reverse = -face_courant
    backward = face_courant * (section(left_edge, 1, 0, axis) + 0.5 * reverse * (section(slope, 1, 0, axis) + (1.0 - 2.0 / 3.0 * reverse) * section(curve, 1, 0, axis)))
    crossing = jnp.where(face_courant >= 0, upwind, backward)
    return section(values, 3, -3, axis) - (section(crossing, 1, 0, axis) - section(crossing, 0, -1, axis))


def wrap_lon(values):
    return jnp.concatenate([values[..., -3:], values, values[..., :3]], axis=3)


def pad_lat(values):
    return jnp.pad(values, ((0, 0), (0, 0), (3, 3), (0, 0)))


def reference(features, land_tile, land_spot, w_in, b_in, w_mid, b_mid, w_out, tracers, zonal_wind, meridional_wind, mixing):
    first = jax.nn.silu(jnp.dot(features, w_in, preferred_element_type=jnp.float32) + b_in).astype(jnp.bfloat16)
    second = jax.nn.silu(jnp.dot(first, w_mid, preferred_element_type=jnp.float32) + b_mid).astype(jnp.bfloat16)
    surface_flux = jnp.dot(second, w_out, preferred_element_type=jnp.float32)
    owner_tile = land_tile[:, 0].astype(jnp.int32)
    spot_index = land_spot.astype(jnp.int32)
    grid_rows = (owner_tile // N_LON) * CLAT + spot_index // CLON
    grid_cols = (owner_tile % N_LON) * CLON + spot_index % CLON
    emitted = jnp.zeros((TR, NLAT, NLON), jnp.float32).at[:, grid_rows, grid_cols].add(surface_flux.T)
    northern = (jnp.arange(NLAT) < NLAT - 1).astype(jnp.float32)
    meridional = (meridional_wind * northern[None, :, None])[None]
    zonal = zonal_wind[None]
    zonal_wide = wrap_lon(zonal)
    meridional_wide = pad_lat(meridional)

    def column(pair):
        state, source = pair
        state = state.at[0].add(source)[None]
        for substep in range(SUBSTEPS):
            state = transport(wrap_lon(state), zonal_wide, 3)
        for substep in range(SUBSTEPS):
            state = transport(pad_lat(state), meridional_wide, 2)
        return jnp.einsum('akj,jab->kab', mixing, state[0], precision=lax.Precision.HIGHEST)

    return lax.map(column, (tracers, emitted))
```

```python
import functools

import jax
import jax.numpy as jnp
from jax import lax
from jax.experimental import pallas as pl
from jax.experimental.pallas import tpu as pltpu
from jax.sharding import PartitionSpec as P

MESH = pl.DeviceIdType.MESH
LANES = 128
WIDE = 6


def silu(v):
    return v / (1.0 + jnp.exp(-v))


def face_weights(c):
    p = jnp.maximum(c, 0.0)
    w = jnp.maximum(-c, 0.0)
    alpha = 0.5 * p * p
    beta = 1.0 - 2.0 / 3.0 * p
    gamma = 0.5 * w * w
    delta = 1.0 - 2.0 / 3.0 * w
    x = alpha * (1.0 - 3.0 * beta)
    y = c - alpha * (1.0 + 3.0 * beta) + gamma * (1.0 + 3.0 * delta)
    z = -gamma * (1.0 - 3.0 * delta)
    u = 6.0 * alpha * beta
    v = -6.0 * gamma * delta
    a, b = 7.0 / 12.0, 1.0 / 12.0
    return [
        -b * x,
        a * x - b * y,
        a * (x + y) - b * z + u,
        a * (y + z) - b * x + v,
        a * z - b * y,
        -b * z,
    ]


def cell_weights(c, before):
    f, g = face_weights(c), face_weights(before)
    out = [g[0]]
    for m in range(5):
        out.append(g[m + 1] - f[m])
    out.append(-f[5])
    out[3] = out[3] + 1.0
    return out


def kernel(
    n_lat,
    n_lon,
    cap,
    feat_ref,
    tile_ref,
    spot_ref,
    w_in_ref,
    b_in_ref,
    w_mid_ref,
    b_mid_ref,
    w_out_ref,
    x_ref,
    zon_ref,
    mer_ref,
    mix_ref,
    out_ref,
    lon_out,
    lon_in,
    lon0_out,
    lon0_in,
    mer_in,
    route_out,
    route_in,
    gz,
    gze,
    gm,
    st,
    fin,
    lon_sem,
    lon0_sem,
    mer_sem,
    route_send,
    route_recv,
    lat_send,
    lat_recv,
):
    lev, rows, _ = zon_ref.shape
    cells = feat_ref.shape[0]
    tr = st.shape[2]
    per = lev * rows
    count = n_lat * n_lon
    groups = LANES // cap
    blocks = count // groups
    lat, lon = lax.axis_index("lat"), lax.axis_index("lon")
    me = lat * n_lon + lon
    west, east = lax.rem(lon + n_lon - 1, n_lon), lax.rem(lon + 1, n_lon)
    has_south, has_north = lat > 0, lat < n_lat - 1

    def place(d):
        return lax.rem(d, groups) * blocks + d // groups

    barrier = pltpu.get_barrier_semaphore()

    @pl.loop(1, count)
    def _(o):
        d = lax.rem(me + o, count)
        pl.semaphore_signal(
            barrier, inc=1, device_id=(d // n_lon, lax.rem(d, n_lon)), device_id_type=MESH
        )

    lane = lax.broadcasted_iota(jnp.int32, (tr, LANES), 1)
    lane8 = lax.broadcasted_iota(jnp.int32, (rows, LANES), 1)

    def column(k, a):
        return x_ref[pl.ds(k * rows + a, tr, stride=per), :]

    @pl.loop(0, lev // 2)
    def _(kp):
        left = jnp.zeros((tr, LANES), jnp.float32)
        right = left
        for p in range(2 * rows):
            q = column(2 * kp + p // rows, p % rows)
            mine = lane // 8 == p
            left = jnp.where(mine, pltpu.roll(q, 8 * p, 1), left)
            right = jnp.where(mine, pltpu.roll(q, (8 * p + 8) % LANES, 1), right)
        lon_out[0, pl.ds(2 * kp, 2)] = left.reshape(2, 8, LANES)
        lon_out[1, pl.ds(2 * kp, 2)] = right.reshape(2, 8, LANES)

    left = jnp.zeros((rows, LANES), jnp.float32)
    right = left
    for k in range(lev):
        c = zon_ref[k]
        mine = lane8 // 8 == k
        left = jnp.where(mine, pltpu.roll(c, (8 * k) % LANES, 1), left)
        right = jnp.where(mine, pltpu.roll(c, (8 * k + 8) % LANES, 1), right)
    lon_out[0, lev] = left
    lon_out[1, lev] = right

    pl.semaphore_wait(barrier, count - 1)

    def lon_copy(side):
        return pltpu.make_async_remote_copy(
            src_ref=lon_out.at[side],
            dst_ref=lon_in.at[side],
            send_sem=lon_sem.at[0, side],
            recv_sem=lon_sem.at[1, side],
            device_id=(lat, (west, east)[side]),
            device_id_type=MESH,
        )

    def lon0_copy(side):
        return pltpu.make_async_remote_copy(
            src_ref=lon0_out.at[side],
            dst_ref=lon0_in.at[side],
            send_sem=lon0_sem.at[0, side],
            recv_sem=lon0_sem.at[1, side],
            device_id=(lat, (west, east)[side]),
            device_id_type=MESH,
        )

    def mer_copy(side):
        return pltpu.make_async_remote_copy(
            src_ref=mer_ref,
            dst_ref=mer_in.at[side],
            send_sem=mer_sem.at[0, side],
            recv_sem=mer_sem.at[1, side],
            device_id=(lat + (-1, 1)[side], lon),
            device_id_type=MESH,
        )

    def lat_copy(k, side):
        return pltpu.make_async_remote_copy(
            src_ref=st.at[k, pl.ds((WIDE, rows)[side], WIDE)],
            dst_ref=st.at[k, pl.ds((WIDE + rows, 0)[side], WIDE)],
            send_sem=lat_send.at[side, k],
            recv_sem=lat_recv.at[side, k],
            device_id=(lat + (-1, 1)[side], lon),
            device_id_type=MESH,
        )

    def route_copy(d, origin):
        return pltpu.make_async_remote_copy(
            src_ref=route_out.at[place(d)],
            dst_ref=route_in.at[place(origin)],
            send_sem=route_send.at[d],
            recv_sem=route_recv.at[origin],
            device_id=(d // n_lon, lax.rem(d, n_lon)),
            device_id_type=MESH,
        )

    lon_copy(0).start()
    lon_copy(1).start()

    @pl.when(has_south)
    def _():
        mer_copy(0).start()

    @pl.when(has_north)
    def _():
        mer_copy(1).start()

    @pl.when(jnp.logical_not(has_south))
    def _():
        mer_in[1] = jnp.zeros((lev, rows, LANES), jnp.float32)

        @pl.loop(0, lev)
        def _(k):
            st[k, 0:WIDE] = jnp.zeros((WIDE, tr, LANES), jnp.float32)

    @pl.when(jnp.logical_not(has_north))
    def _():
        mer_in[0] = jnp.zeros((lev, rows, LANES), jnp.float32)

        @pl.loop(0, lev)
        def _(k):
            st[k, WIDE + rows :] = jnp.zeros((WIDE, tr, LANES), jnp.float32)

    first = silu(
        jnp.dot(feat_ref[...], w_in_ref[...], preferred_element_type=jnp.float32) + b_in_ref[...]
    ).astype(jnp.bfloat16)
    second = silu(
        jnp.dot(first, w_mid_ref[...], preferred_element_type=jnp.float32) + b_mid_ref[...]
    ).astype(jnp.bfloat16)
    flux = lax.dot_general(
        w_out_ref[...], second, (((0,), (1,)), ((), ())), preferred_element_type=jnp.float32
    )

    tile = tile_ref[...]
    named = (tile == lax.broadcasted_iota(jnp.int32, (cells, LANES), 1)).astype(jnp.float32)
    ahead = (
        lax.broadcasted_iota(jnp.int32, (cells, cells), 0)
        > lax.broadcasted_iota(jnp.int32, (cells, cells), 1)
    ).astype(jnp.float32)
    rank = jnp.dot(
        ahead.astype(jnp.bfloat16), named.astype(jnp.bfloat16), preferred_element_type=jnp.float32
    )
    slot = jnp.sum(rank * named, axis=1, keepdims=True).astype(jnp.int32)
    key = tile * cap + slot
    taken = (key == lax.broadcasted_iota(jnp.int32, (cells, count * cap), 1)).astype(jnp.float32)
    spot = spot_ref[...]
    spots = jnp.where(
        lax.broadcasted_iota(jnp.int32, (16, cells), 0) == 0, spot // LANES, spot % LANES
    ).astype(jnp.float32)
    high = flux.astype(jnp.bfloat16)
    low = (flux - high.astype(jnp.float32)).astype(jnp.bfloat16)
    parts = jnp.concatenate([high, low, spots.astype(jnp.bfloat16)], axis=0)
    placed = jnp.dot(parts, taken.astype(jnp.bfloat16), preferred_element_type=jnp.float32)
    summed = placed[0:tr] + placed[tr : 2 * tr]
    pieces = [summed[0:8], summed[8:16], placed[2 * tr : 2 * tr + 8]]
    stacked = [
        jnp.concatenate([piece[:, LANES * j : LANES * (j + 1)] for j in range(blocks)], axis=0)
        for piece in pieces
    ]
    laneb = lax.broadcasted_iota(jnp.int32, (8 * blocks, LANES), 1)
    for g in range(groups):
        turned = [
            pltpu.roll(s, (cap * (h - g)) % LANES, 1) if h != g else s
            for h, s in enumerate(stacked)
        ]
        packed = jnp.where(laneb < cap, turned[0], jnp.where(laneb < 2 * cap, turned[1], turned[2]))
        route_out[blocks * g : blocks * (g + 1)] = packed.reshape(blocks, 8, LANES)

    @pl.loop(1, count)
    def _(o):
        route_copy(lax.rem(me + o, count), me).start()

    route_in[place(me)] = route_out[place(me)]

    lon_copy(0).wait_recv()
    lon_copy(1).wait_recv()

    def ring(main, ext, m, where):
        if m == 0:
            return main, ext
        if m > 0:
            mask, turn = where < m, LANES - m
        else:
            mask, turn = where >= LANES + m, -m
        return (
            pltpu.roll(jnp.where(mask, ext, main), turn, 1),
            pltpu.roll(jnp.where(mask, main, ext), turn, 1),
        )

    def unpack(from_west, from_east, p, where):
        return jnp.where(
            where < 8,
            pltpu.roll(from_east, (LANES - 8 * p) % LANES, 1),
            pltpu.roll(from_west, (LANES - 8 - 8 * p) % LANES, 1),
        )

    for k in range(lev):
        c = zon_ref[k]
        ce = unpack(lon_in[1, lev], lon_in[0, lev], k, lane8)
        before, before_e = ring(c, ce, -1, lane8)
        for m, weight in enumerate(cell_weights(c, before)):
            gz[k, m] = weight
        for m, weight in enumerate(cell_weights(ce, before_e)):
            gze[k, m] = weight

    def zonal(k, a, main, ext):
        new, new_e = 0.0, 0.0
        for m in range(-3, 4):
            near, near_e = ring(main, ext, m, lane)
            new = new + near * gz[k, m + 3, a : a + 1, :]
            new_e = new_e + near_e * gze[k, m + 3, a : a + 1, :]
        main, ext = new, new_e
        new = 0.0
        for m in range(-3, 4):
            if m == 0:
                near = main
            elif m > 0:
                near = pltpu.roll(jnp.where(lane < m, ext, main), LANES - m, 1)
            else:
                near = pltpu.roll(jnp.where(lane >= LANES + m, ext, main), -m, 1)
            new = new + near * gz[k, m + 3, a : a + 1, :]
        st[k, WIDE + a] = new

    def send_rows(k):
        @pl.when(has_south)
        def _():
            lat_copy(k, 0).start()

        @pl.when(has_north)
        def _():
            lat_copy(k, 1).start()

    def pair(kp, parities):
        from_west = lon_in[1, pl.ds(2 * kp, 2)].reshape(tr, LANES)
        from_east = lon_in[0, pl.ds(2 * kp, 2)].reshape(tr, LANES)
        for parity in parities:
            k = 2 * kp + parity
            for a in range(rows):
                ext = unpack(from_west, from_east, parity * rows + a, lane)
                zonal(k, a, column(k, a), ext)
            send_rows(k)

    pair(0, (1,))

    @pl.loop(1, lev // 2)
    def _(kp):
        pair(kp, (0, 1))

    @pl.loop(1, count)
    def _(o):
        route_copy(me, lax.rem(me + o, count)).wait_recv()

    lists = [jnp.zeros((8 * blocks, LANES), jnp.float32)] * 3
    for g in range(groups):
        got = route_in[blocks * g : blocks * (g + 1)].reshape(8 * blocks, LANES)
        for h in range(3):
            turned = pltpu.roll(got, (cap * (g - h)) % LANES, 1) if g != h else got
            lists[h] = jnp.where(laneb // cap == g, turned, lists[h])
    entries = [
        jnp.concatenate([part[8 * j : 8 * (j + 1)] for j in range(blocks)], axis=1)
        for part in lists
    ]
    values = jnp.concatenate(entries[:2], axis=0)
    at_row, at_lane = entries[2][0:1], entries[2][1:2]
    wide = blocks * LANES
    onto = (
        lax.broadcasted_iota(jnp.int32, (LANES, wide), 0).astype(jnp.float32) == at_lane
    ).astype(jnp.float32)
    spread = jnp.concatenate(
        [jnp.where(at_row == float(a), values, 0.0) for a in range(rows)], axis=0
    )
    high = spread.astype(jnp.bfloat16)
    low = (spread - high.astype(jnp.float32)).astype(jnp.bfloat16)
    emitted = lax.dot_general(
        jnp.concatenate([high, low], axis=0),
        onto.astype(jnp.bfloat16),
        (((1,), (1,)), ((), ())),
        preferred_element_type=jnp.float32,
    )
    emitted = emitted[: rows * tr] + emitted[rows * tr :]

    surface = [column(0, a) + emitted[a * tr : (a + 1) * tr] for a in range(rows)]
    left = jnp.zeros((tr, LANES), jnp.float32)
    right = left
    for a in range(rows):
        mine = lane // 8 == a
        left = jnp.where(mine, pltpu.roll(surface[a], 8 * a, 1), left)
        right = jnp.where(mine, pltpu.roll(surface[a], 8 * a + 8, 1), right)
        fin[0, a] = surface[a]
    lon0_out[0] = left
    lon0_out[1] = right
    lon0_copy(0).start()
    lon0_copy(1).start()

    @pl.when(has_south)
    def _():
        mer_copy(1).wait_recv()

    @pl.when(has_north)
    def _():
        mer_copy(0).wait_recv()

    grid_row = lax.broadcasted_iota(jnp.int32, (3 * rows, LANES), 0) + (lat - 1) * rows
    northern = (grid_row < n_lat * rows - 1).astype(jnp.float32)

    @pl.loop(0, lev)
    def _(k):
        c = jnp.concatenate([mer_in[1, k], mer_ref[k], mer_in[0, k]], axis=0) * northern
        for m, weight in enumerate(cell_weights(c, pltpu.roll(c, 1, 0))):
            gm[k, m] = weight

    lon0_copy(0).wait_recv()
    lon0_copy(1).wait_recv()
    for a in range(rows):
        zonal(0, a, fin[0, a], unpack(lon0_in[1], lon0_in[0], a, lane))
    send_rows(0)

    def meridional(k):
        @pl.when(has_south)
        def _():
            lat_copy(k, 1).wait_recv()

        @pl.when(has_north)
        def _():
            lat_copy(k, 0).wait_recv()

        for h in range(0, tr, 8):
            once = []
            for a in range(-3, rows + 3):
                new = 0.0
                for m in range(7):
                    new = new + st[k, a + 3 + m, h : h + 8] * gm[k, m, a + rows : a + rows + 1]
                once.append(new)
            for a in range(rows):
                new = 0.0
                for m in range(7):
                    new = new + once[a + m] * gm[k, m, a + rows : a + rows + 1]
                fin[k, a, h : h + 8] = new

    @pl.loop(1, lev)
    def _(k):
        meridional(k)

    meridional(0)

    @pl.loop(0, rows)
    def _(a):
        for h in range(0, tr, 8):
            held = [fin[j, a, h : h + 8] for j in range(lev)]
            for k in range(lev):
                total = held[0] * mix_ref[a, k, 0]
                for j in range(1, lev):
                    total = total + held[j] * mix_ref[a, k, j]
                out_ref[pl.ds(h * per + k * rows + a, 8, stride=per), :] = total

    for side in range(2):
        lon_copy(side).wait_send()
        lon0_copy(side).wait_send()

    @pl.loop(1, count)
    def _(o):
        route_copy(lax.rem(me + o, count), me).wait_send()

    @pl.when(has_south)
    def _():
        mer_copy(0).wait_send()

        @pl.loop(0, lev)
        def _(k):
            lat_copy(k, 0).wait_send()

    @pl.when(has_north)
    def _():
        mer_copy(1).wait_send()

        @pl.loop(0, lev)
        def _(k):
            lat_copy(k, 1).wait_send()


def on_device(
    n_lat,
    n_lon,
    features,
    land_tile,
    land_spot,
    w_in,
    b_in,
    w_mid,
    b_mid,
    w_out,
    tracers,
    zonal_wind,
    meridional_wind,
    mixing,
):
    tr, lev, rows, cols = tracers.shape
    cells = features.shape[0]
    count = n_lat * n_lon
    cap = 2 * cells // count
    f32 = jnp.float32
    vmem = pl.BlockSpec(memory_space=pltpu.VMEM)
    smem = pl.BlockSpec(memory_space=pltpu.SMEM)
    out = pl.pallas_call(
        functools.partial(kernel, n_lat, n_lon, cap),
        out_shape=jax.ShapeDtypeStruct((tr * lev * rows, cols), f32),
        in_specs=[vmem] * 11 + [smem],
        out_specs=vmem,
        scratch_shapes=[
            pltpu.VMEM((2, lev + 1, 8, cols), f32),
            pltpu.VMEM((2, lev + 1, 8, cols), f32),
            pltpu.VMEM((2, tr, cols), f32),
            pltpu.VMEM((2, tr, cols), f32),
            pltpu.VMEM((2, lev, rows, cols), f32),
            pltpu.VMEM((count, 8, cols), f32),
            pltpu.VMEM((count, 8, cols), f32),
            pltpu.VMEM((lev, 7, rows, cols), f32),
            pltpu.VMEM((lev, 7, rows, cols), f32),
            pltpu.VMEM((lev, 7, 3 * rows, cols), f32),
            pltpu.VMEM((lev, rows + 2 * WIDE, tr, cols), f32),
            pltpu.VMEM((lev, rows, tr, cols), f32),
            pltpu.SemaphoreType.DMA((2, 2)),
            pltpu.SemaphoreType.DMA((2, 2)),
            pltpu.SemaphoreType.DMA((2, 2)),
            pltpu.SemaphoreType.DMA((count,)),
            pltpu.SemaphoreType.DMA((count,)),
            pltpu.SemaphoreType.DMA((2, lev)),
            pltpu.SemaphoreType.DMA((2, lev)),
        ],
        compiler_params=pltpu.CompilerParams(
            collective_id=0, has_side_effects=True, vmem_limit_bytes=40 * 1024 * 1024
        ),
    )(
        features,
        land_tile,
        land_spot.reshape(1, -1),
        w_in,
        b_in.reshape(1, -1),
        w_mid,
        b_mid.reshape(1, -1),
        w_out,
        tracers.reshape(tr * lev * rows, cols),
        zonal_wind,
        meridional_wind,
        mixing,
    )
    return out.reshape(tr, lev, rows, cols)


def solution(mesh):
    placed = (
        P(("lat", "lon"), None),
        P(("lat", "lon"), None),
        P(("lat", "lon")),
        P(),
        P(),
        P(),
        P(),
        P(),
        P(None, None, "lat", "lon"),
        P(None, "lat", "lon"),
        P(None, "lat", "lon"),
        P("lat", None, None),
    )
    return jax.shard_map(
        functools.partial(on_device, mesh.shape["lat"], mesh.shape["lon"]),
        mesh=mesh,
        in_specs=placed,
        out_specs=P(None, None, "lat", "lon"),
        check_vma=False,
    )
```

```python
import functools

import jax
import jax.numpy as jnp
from jax import lax
from jax.experimental import pallas as pl
from jax.experimental.pallas import tpu as pltpu
from jax.sharding import PartitionSpec as P

MESH = pl.DeviceIdType.MESH
LANES = 128
WIDE = 6


def silu(v):
    return v / (1.0 + jnp.exp(-v))


def face_weights(c):
    p = jnp.maximum(c, 0.0)
    w = jnp.maximum(-c, 0.0)
    alpha = 0.5 * p * p
    beta = 1.0 - 2.0 / 3.0 * p
    gamma = 0.5 * w * w
    delta = 1.0 - 2.0 / 3.0 * w
    x = alpha * (1.0 - 3.0 * beta)
    y = c - alpha * (1.0 + 3.0 * beta) + gamma * (1.0 + 3.0 * delta)
    z = -gamma * (1.0 - 3.0 * delta)
    u = 6.0 * alpha * beta
    v = -6.0 * gamma * delta
    a, b = 7.0 / 12.0, 1.0 / 12.0
    return [
        -b * x,
        a * x - b * y,
        a * (x + y) - b * z + u,
        a * (y + z) - b * x + v,
        a * z - b * y,
        -b * z,
    ]


def cell_weights(c, before):
    f, g = face_weights(c), face_weights(before)
    out = [g[0]]
    for m in range(5):
        out.append(g[m + 1] - f[m])
    out.append(-f[5])
    out[3] = out[3] + 1.0
    return out


def kernel(
    n_lat,
    n_lon,
    cap,
    *refs,
):
    given, refs = refs[:12], refs[12:]
    out_ref, held, refs = refs[0], refs[1:13], refs[13:]
    transport_step(n_lat, n_lon, cap, given, held, out_ref, *refs)


def transport_step(
    n_lat,
    n_lon,
    cap,
    given,
    held,
    out_ref,
    given_sem,
    lon_out,
    lon_in,
    lon0_out,
    lon0_in,
    mer_in,
    route_out,
    route_in,
    gz,
    gze,
    gm,
    st,
    fin,
    acc,
    slots,
    lon_sem,
    lon0_sem,
    mer_sem,
    route_send,
    route_recv,
    lat_send,
    lat_recv,
):
    (
        feat_ref,
        tile_ref,
        spot_ref,
        w_in_ref,
        b_in_ref,
        w_mid_ref,
        b_mid_ref,
        w_out_ref,
        x_ref,
        zon_ref,
        mer_ref,
        mix_ref,
    ) = held
    lev, rows, _ = zon_ref.shape
    cells = feat_ref.shape[1]
    tr = st.shape[2]
    per = lev * rows
    count = n_lat * n_lon
    groups = LANES // cap
    blocks = count // groups
    lat, lon = lax.axis_index("lat"), lax.axis_index("lon")
    me = lat * n_lon + lon
    west, east = lax.rem(lon + n_lon - 1, n_lon), lax.rem(lon + 1, n_lon)
    has_south, has_north = lat > 0, lat < n_lat - 1

    def place(d):
        return lax.rem(d, groups) * blocks + d // groups

    def load(i):
        return pltpu.make_async_copy(given[i], held[i], given_sem.at[i])

    for i in (8, 9, 10, 0, 3, 5, 4, 6, 7, 1, 2, 11):
        load(i).start()

    barrier = pltpu.get_barrier_semaphore()

    @pl.loop(1, count)
    def _(o):
        d = lax.rem(me + o, count)
        pl.semaphore_signal(
            barrier, inc=1, device_id=(d // n_lon, lax.rem(d, n_lon)), device_id_type=MESH
        )

    lane = lax.broadcasted_iota(jnp.int32, (tr, LANES), 1)
    lane8 = lax.broadcasted_iota(jnp.int32, (rows, LANES), 1)

    def column(k, a):
        return x_ref[pl.ds(k * rows + a, tr, stride=per), :]

    @pl.when(jnp.logical_not(has_south))
    def _():
        mer_in[1] = jnp.zeros((lev, rows, LANES), jnp.float32)

        @pl.loop(0, lev)
        def _(k):
            st[k, 0:WIDE] = jnp.zeros((WIDE, tr, LANES), jnp.float32)

    @pl.when(jnp.logical_not(has_north))
    def _():
        mer_in[0] = jnp.zeros((lev, rows, LANES), jnp.float32)

        @pl.loop(0, lev)
        def _(k):
            st[k, WIDE + rows :] = jnp.zeros((WIDE, tr, LANES), jnp.float32)

    load(8).wait()

    @pl.loop(0, lev // 2)
    def _(kp):
        left = jnp.zeros((tr, LANES), jnp.float32)
        right = left
        for p in range(2 * rows):
            q = column(2 * kp + p // rows, p % rows)
            st[2 * kp + p // rows, WIDE + p % rows] = q
            mine = lane // 8 == p
            left = jnp.where(mine, pltpu.roll(q, 8 * p, 1), left)
            right = jnp.where(mine, pltpu.roll(q, (8 * p + 8) % LANES, 1), right)
        lon_out[0, pl.ds(2 * kp, 2)] = left.reshape(2, 8, LANES)
        lon_out[1, pl.ds(2 * kp, 2)] = right.reshape(2, 8, LANES)

    load(9).wait()
    left = jnp.zeros((rows, LANES), jnp.float32)
    right = left
    for k in range(lev):
        c = zon_ref[k]
        mine = lane8 // 8 == k
        left = jnp.where(mine, pltpu.roll(c, (8 * k) % LANES, 1), left)
        right = jnp.where(mine, pltpu.roll(c, (8 * k + 8) % LANES, 1), right)
    lon_out[0, lev] = left
    lon_out[1, lev] = right

    pl.semaphore_wait(barrier, count - 1)

    def lon_copy(side):
        return pltpu.make_async_remote_copy(
            src_ref=lon_out.at[side],
            dst_ref=lon_in.at[side],
            send_sem=lon_sem.at[0, side],
            recv_sem=lon_sem.at[1, side],
            device_id=(lat, (west, east)[side]),
            device_id_type=MESH,
        )

    def lon0_copy(side):
        return pltpu.make_async_remote_copy(
            src_ref=lon0_out.at[side],
            dst_ref=lon0_in.at[side],
            send_sem=lon0_sem.at[0, side],
            recv_sem=lon0_sem.at[1, side],
            device_id=(lat, (west, east)[side]),
            device_id_type=MESH,
        )

    def mer_copy(side):
        return pltpu.make_async_remote_copy(
            src_ref=mer_ref,
            dst_ref=mer_in.at[side],
            send_sem=mer_sem.at[0, side],
            recv_sem=mer_sem.at[1, side],
            device_id=(lat + (-1, 1)[side], lon),
            device_id_type=MESH,
        )

    def lat_copy(k, side):
        return pltpu.make_async_remote_copy(
            src_ref=st.at[k, pl.ds((WIDE, rows)[side], WIDE)],
            dst_ref=st.at[k, pl.ds((WIDE + rows, 0)[side], WIDE)],
            send_sem=lat_send.at[side, k],
            recv_sem=lat_recv.at[side, k],
            device_id=(lat + (-1, 1)[side], lon),
            device_id_type=MESH,
        )

    def route_copy(d, origin):
        return pltpu.make_async_remote_copy(
            src_ref=route_out.at[place(d)],
            dst_ref=route_in.at[place(origin)],
            send_sem=route_send.at[d],
            recv_sem=route_recv.at[origin],
            device_id=(d // n_lon, lax.rem(d, n_lon)),
            device_id_type=MESH,
        )

    lon_copy(0).start()
    lon_copy(1).start()
    load(10).wait()

    @pl.when(has_south)
    def _():
        mer_copy(0).start()

    @pl.when(has_north)
    def _():
        mer_copy(1).start()

    for i in (0, 3, 5, 4, 6, 7, 1, 2):
        load(i).wait()
    first = silu(
        lax.dot_general(
            feat_ref[...], w_in_ref[...], (((0,), (0,)), ((), ())), preferred_element_type=jnp.float32
        )
        + b_in_ref[...]
    ).astype(jnp.bfloat16)
    second = silu(
        jnp.dot(first, w_mid_ref[...], preferred_element_type=jnp.float32) + b_mid_ref[...]
    ).astype(jnp.bfloat16)
    flux = lax.dot_general(
        w_out_ref[...], second, (((1,), (1,)), ((), ())), preferred_element_type=jnp.float32
    )

    lon_copy(0).wait_recv()
    lon_copy(1).wait_recv()

    def ring(main, ext, m, where):
        if m == 0:
            return main, ext
        if m > 0:
            mask, turn = where < m, LANES - m
        else:
            mask, turn = where >= LANES + m, -m
        return (
            pltpu.roll(jnp.where(mask, ext, main), turn, 1),
            pltpu.roll(jnp.where(mask, main, ext), turn, 1),
        )

    def unpack(from_west, from_east, p, where):
        return jnp.where(
            where < 8,
            pltpu.roll(from_east, (LANES - 8 * p) % LANES, 1),
            pltpu.roll(from_west, (LANES - 8 - 8 * p) % LANES, 1),
        )

    @pl.loop(0, lev)
    def _(k):
        c = zon_ref[k]
        ce = jnp.where(
            lane8 < 8,
            pltpu.roll(lon_in[0, lev], lax.rem(LANES - 8 * k, LANES), 1),
            pltpu.roll(lon_in[1, lev], LANES - 8 - 8 * k, 1),
        )
        before, before_e = ring(c, ce, -1, lane8)
        for m, weight in enumerate(cell_weights(c, before)):
            gz[k, m] = weight
        for m, weight in enumerate(cell_weights(ce, before_e)):
            gze[k, m] = weight

    def zonal(k, a, main, ext):
        new, new_e = 0.0, 0.0
        for m in range(-3, 4):
            near, near_e = ring(main, ext, m, lane)
            new = new + near * gz[k, m + 3, a : a + 1, :]
            new_e = new_e + near_e * gze[k, m + 3, a : a + 1, :]
        main, ext = new, new_e
        new = 0.0
        for m in range(-3, 4):
            if m == 0:
                near = main
            elif m > 0:
                near = pltpu.roll(jnp.where(lane < m, ext, main), LANES - m, 1)
            else:
                near = pltpu.roll(jnp.where(lane >= LANES + m, ext, main), -m, 1)
            new = new + near * gz[k, m + 3, a : a + 1, :]
        st[k, WIDE + a] = new

    def send_rows(k):
        @pl.when(has_south)
        def _():
            lat_copy(k, 0).start()

        @pl.when(has_north)
        def _():
            lat_copy(k, 1).start()

    def pair(kp, parities):
        from_west = lon_in[1, pl.ds(2 * kp, 2)].reshape(tr, LANES)
        from_east = lon_in[0, pl.ds(2 * kp, 2)].reshape(tr, LANES)
        for parity in parities:
            k = 2 * kp + parity
            for a in range(rows):
                ext = unpack(from_west, from_east, parity * rows + a, lane)
                zonal(k, a, st[k, WIDE + a], ext)
            send_rows(k)

    pair(0, (1,))

    @pl.loop(1, lev // 4)
    def _(kp):
        pair(kp, (0, 1))

    tile = tile_ref[...]
    named = (tile == lax.broadcasted_iota(jnp.int32, (count, cells), 0)).astype(jnp.float32)
    ahead = (
        lax.broadcasted_iota(jnp.int32, (cells, cells), 0)
        < lax.broadcasted_iota(jnp.int32, (cells, cells), 1)
    ).astype(jnp.float32)
    rank = jnp.dot(
        named.astype(jnp.bfloat16), ahead.astype(jnp.bfloat16), preferred_element_type=jnp.float32
    )
    slot = jnp.sum(rank * named, axis=0, keepdims=True).astype(jnp.int32)
    key = tile * cap + slot
    spot = spot_ref[...]
    spots = jnp.where(
        lax.broadcasted_iota(jnp.int32, (16, cells), 0) == 0, spot // LANES, spot % LANES
    ).astype(jnp.float32)
    high = flux.astype(jnp.bfloat16)
    low = (flux - high.astype(jnp.float32)).astype(jnp.bfloat16)
    parts = jnp.concatenate([high, low, spots.astype(jnp.bfloat16)], axis=0)
    lane_of = lax.broadcasted_iota(jnp.int32, (LANES, cells), 0)

    @pl.loop(0, blocks)
    def _(j):
        taken = (key - j * LANES == lane_of).astype(jnp.float32).astype(jnp.bfloat16)
        placed = lax.dot_general(
            parts, taken, (((1,), (1,)), ((), ())), preferred_element_type=jnp.float32
        )
        summed = placed[0:tr] + placed[tr : 2 * tr]
        slots[0, j] = summed[0:8]
        slots[1, j] = summed[8:16]
        slots[2, j] = placed[2 * tr : 2 * tr + 8]

    stacked = [slots[h].reshape(8 * blocks, LANES) for h in range(3)]
    laneb = lax.broadcasted_iota(jnp.int32, (8 * blocks, LANES), 1)
    for g in range(groups):
        turned = [
            pltpu.roll(s, (cap * (h - g)) % LANES, 1) if h != g else s
            for h, s in enumerate(stacked)
        ]
        packed = jnp.where(laneb < cap, turned[0], jnp.where(laneb < 2 * cap, turned[1], turned[2]))
        route_out[blocks * g : blocks * (g + 1)] = packed.reshape(blocks, 8, LANES)

    @pl.loop(1, count)
    def _(o):
        route_copy(lax.rem(me + o, count), me).start()

    route_in[place(me)] = route_out[place(me)]

    @pl.loop(lev // 4, lev // 2)
    def _(kp):
        pair(kp, (0, 1))

    @pl.when(has_south)
    def _():
        mer_copy(1).wait_recv()

    @pl.when(has_north)
    def _():
        mer_copy(0).wait_recv()

    grid_row = lax.broadcasted_iota(jnp.int32, (3 * rows, LANES), 0) + (lat - 1) * rows
    northern = (grid_row < n_lat * rows - 1).astype(jnp.float32)

    @pl.loop(0, lev)
    def _(k):
        c = jnp.concatenate([mer_in[1, k], mer_ref[k], mer_in[0, k]], axis=0) * northern
        for m, weight in enumerate(cell_weights(c, pltpu.roll(c, 1, 0))):
            gm[k, m] = weight

    @pl.loop(1, count)
    def _(o):
        route_copy(me, lax.rem(me + o, count)).wait_recv()

    lists = [jnp.zeros((8 * blocks, LANES), jnp.float32)] * 3
    for g in range(groups):
        got = route_in[blocks * g : blocks * (g + 1)].reshape(8 * blocks, LANES)
        for h in range(3):
            turned = pltpu.roll(got, (cap * (g - h)) % LANES, 1) if g != h else got
            lists[h] = jnp.where(laneb // cap == g, turned, lists[h])
    entries = [
        jnp.concatenate([part[8 * j : 8 * (j + 1)] for j in range(blocks)], axis=1)
        for part in lists
    ]
    values = jnp.concatenate(entries[:2], axis=0)
    at_row, at_lane = entries[2][0:1], entries[2][1:2]
    wide = blocks * LANES
    onto = (
        lax.broadcasted_iota(jnp.int32, (LANES, wide), 0).astype(jnp.float32) == at_lane
    ).astype(jnp.float32)
    spread = jnp.concatenate(
        [jnp.where(at_row == float(a), values, 0.0) for a in range(rows)], axis=0
    )
    high = spread.astype(jnp.bfloat16)
    low = (spread - high.astype(jnp.float32)).astype(jnp.bfloat16)
    emitted = lax.dot_general(
        jnp.concatenate([high, low], axis=0),
        onto.astype(jnp.bfloat16),
        (((1,), (1,)), ((), ())),
        preferred_element_type=jnp.float32,
    )
    emitted = emitted[: rows * tr] + emitted[rows * tr :]

    surface = [st[0, WIDE + a] + emitted[a * tr : (a + 1) * tr] for a in range(rows)]
    left = jnp.zeros((tr, LANES), jnp.float32)
    right = left
    for a in range(rows):
        mine = lane // 8 == a
        left = jnp.where(mine, pltpu.roll(surface[a], 8 * a, 1), left)
        right = jnp.where(mine, pltpu.roll(surface[a], 8 * a + 8, 1), right)
        fin[0, a] = surface[a]
    lon0_out[0] = left
    lon0_out[1] = right
    lon0_copy(0).start()
    lon0_copy(1).start()

    def meridional(k):
        @pl.when(has_south)
        def _():
            lat_copy(k, 1).wait_recv()

        @pl.when(has_north)
        def _():
            lat_copy(k, 0).wait_recv()

        once = []
        for a in range(-3, rows + 3):
            new = 0.0
            for m in range(7):
                new = new + st[k, a + 3 + m] * gm[k, m, a + rows : a + rows + 1]
            once.append(new)
        for a in range(rows):
            new = 0.0
            for m in range(7):
                new = new + once[a + m] * gm[k, m, a + rows : a + rows + 1]
            fin[k, a] = new

    def mixed(levels, opening, closing):
        @pl.loop(0, rows)
        def _(a):
            part = [fin[j, a] for j in levels]
            for k in range(lev):
                total = 0.0 if opening else acc[a, k]
                for j, value in zip(levels, part):
                    total = total + value * mix_ref[a, k, j]
                if closing:
                    out_ref[pl.ds(k * rows + a, tr, stride=per), :] = total
                else:
                    acc[a, k] = total

    cuts = [1, 1 + lev // 3, 1 + 2 * (lev // 3), lev]

    def some(i):
        @pl.loop(cuts[i], cuts[i + 1])
        def _(k):
            meridional(k)

        mixed(range(cuts[i], cuts[i + 1]), i == 0, False)

    load(11).wait()
    some(0)
    lon0_copy(0).wait_recv()
    lon0_copy(1).wait_recv()
    for a in range(rows):
        zonal(0, a, fin[0, a], unpack(lon0_in[1], lon0_in[0], a, lane))
    send_rows(0)
    some(1)
    some(2)
    meridional(0)
    mixed(range(1), False, True)

    for side in range(2):
        lon_copy(side).wait_send()
        lon0_copy(side).wait_send()

    @pl.loop(1, count)
    def _(o):
        route_copy(lax.rem(me + o, count), me).wait_send()

    @pl.when(has_south)
    def _():
        mer_copy(0).wait_send()

        @pl.loop(0, lev)
        def _(k):
            lat_copy(k, 0).wait_send()

    @pl.when(has_north)
    def _():
        mer_copy(1).wait_send()

        @pl.loop(0, lev)
        def _(k):
            lat_copy(k, 1).wait_send()


def on_device(
    n_lat,
    n_lon,
    features,
    land_tile,
    land_spot,
    w_in,
    b_in,
    w_mid,
    b_mid,
    w_out,
    tracers,
    zonal_wind,
    meridional_wind,
    mixing,
):
    tr, lev, rows, cols = tracers.shape
    cells = features.shape[0]
    count = n_lat * n_lon
    cap = 2 * cells // count
    f32 = jnp.float32
    args = (
        features.T,
        land_tile.T,
        land_spot.reshape(1, -1),
        w_in,
        b_in.reshape(1, -1),
        w_mid,
        b_mid.reshape(1, -1),
        w_out.T,
        tracers.reshape(tr * lev * rows, cols),
        zonal_wind,
        meridional_wind,
        mixing,
    )
    out = pl.pallas_call(
        functools.partial(kernel, n_lat, n_lon, cap),
        out_shape=jax.ShapeDtypeStruct((tr * lev * rows, cols), f32),
        in_specs=[pl.BlockSpec(memory_space=pltpu.HBM)] * len(args),
        out_specs=pl.BlockSpec(memory_space=pltpu.VMEM),
        scratch_shapes=[pltpu.VMEM(arg.shape, arg.dtype) for arg in args[:-1]]
        + [
            pltpu.SMEM(mixing.shape, f32),
            pltpu.SemaphoreType.DMA((len(args),)),
            pltpu.VMEM((2, lev + 1, 8, cols), f32),
            pltpu.VMEM((2, lev + 1, 8, cols), f32),
            pltpu.VMEM((2, tr, cols), f32),
            pltpu.VMEM((2, tr, cols), f32),
            pltpu.VMEM((2, lev, rows, cols), f32),
            pltpu.VMEM((count, 8, cols), f32),
            pltpu.VMEM((count, 8, cols), f32),
            pltpu.VMEM((lev, 7, rows, cols), f32),
            pltpu.VMEM((lev, 7, rows, cols), f32),
            pltpu.VMEM((lev, 7, 3 * rows, cols), f32),
            pltpu.VMEM((lev, rows + 2 * WIDE, tr, cols), f32),
            pltpu.VMEM((lev, rows, tr, cols), f32),
            pltpu.VMEM((rows, lev, tr, cols), f32),
            pltpu.VMEM((3, count * cap // cols, 8, cols), f32),
            pltpu.SemaphoreType.DMA((2, 2)),
            pltpu.SemaphoreType.DMA((2, 2)),
            pltpu.SemaphoreType.DMA((2, 2)),
            pltpu.SemaphoreType.DMA((count,)),
            pltpu.SemaphoreType.DMA((count,)),
            pltpu.SemaphoreType.DMA((2, lev)),
            pltpu.SemaphoreType.DMA((2, lev)),
        ],
        compiler_params=pltpu.CompilerParams(
            collective_id=0, has_side_effects=True, vmem_limit_bytes=60 * 1024 * 1024
        ),
    )(*args)
    return out.reshape(tr, lev, rows, cols)


def solution(mesh):
    placed = (
        P(("lat", "lon"), None),
        P(("lat", "lon"), None),
        P(("lat", "lon")),
        P(),
        P(),
        P(),
        P(),
        P(),
        P(None, None, "lat", "lon"),
        P(None, "lat", "lon"),
        P(None, "lat", "lon"),
        P("lat", None, None),
    )
    return jax.shard_map(
        functools.partial(on_device, mesh.shape["lat"], mesh.shape["lon"]),
        mesh=mesh,
        in_specs=placed,
        out_specs=P(None, None, "lat", "lon"),
        check_vma=False,
    )
```

```python
import functools

import jax
import jax.numpy as jnp
from jax import lax
from jax.experimental import pallas as pl
from jax.experimental.pallas import tpu as pltpu
from jax.sharding import PartitionSpec as P

MESH = pl.DeviceIdType.MESH
LANES = 128
WIDE = 6


def silu(v):
    return v / (1.0 + jnp.exp(-v))


def face_weights(c):
    p = jnp.maximum(c, 0.0)
    w = jnp.maximum(-c, 0.0)
    alpha = 0.5 * p * p
    beta = 1.0 - 2.0 / 3.0 * p
    gamma = 0.5 * w * w
    delta = 1.0 - 2.0 / 3.0 * w
    x = alpha * (1.0 - 3.0 * beta)
    y = c - alpha * (1.0 + 3.0 * beta) + gamma * (1.0 + 3.0 * delta)
    z = -gamma * (1.0 - 3.0 * delta)
    u = 6.0 * alpha * beta
    v = -6.0 * gamma * delta
    a, b = 7.0 / 12.0, 1.0 / 12.0
    return [
        -b * x,
        a * x - b * y,
        a * (x + y) - b * z + u,
        a * (y + z) - b * x + v,
        a * z - b * y,
        -b * z,
    ]


def cell_weights(c, before):
    f, g = face_weights(c), face_weights(before)
    out = [g[0]]
    for m in range(5):
        out.append(g[m + 1] - f[m])
    out.append(-f[5])
    out[3] = out[3] + 1.0
    return out


def route_kernel(
    n_lat,
    n_lon,
    cap,
    tr,
    rows,
    feat_ref,
    tile_ref,
    spot_ref,
    w_in_ref,
    b_in_ref,
    w_mid_ref,
    b_mid_ref,
    w_out_ref,
    out_ref,
    route_out,
    route_in,
    slots,
    route_send,
    route_recv,
):
    cells = feat_ref.shape[1]
    count = n_lat * n_lon
    groups = LANES // cap
    blocks = count // groups
    lat, lon = lax.axis_index("lat"), lax.axis_index("lon")
    me = lat * n_lon + lon

    def place(d):
        return lax.rem(d, groups) * blocks + d // groups

    barrier = pltpu.get_barrier_semaphore()

    @pl.loop(1, count)
    def _(o):
        d = lax.rem(me + o, count)
        pl.semaphore_signal(
            barrier, inc=1, device_id=(d // n_lon, lax.rem(d, n_lon)), device_id_type=MESH
        )

    first = silu(
        lax.dot_general(
            feat_ref[...], w_in_ref[...], (((0,), (0,)), ((), ())), preferred_element_type=jnp.float32
        )
        + b_in_ref[...]
    ).astype(jnp.bfloat16)
    second = silu(
        jnp.dot(first, w_mid_ref[...], preferred_element_type=jnp.float32) + b_mid_ref[...]
    ).astype(jnp.bfloat16)
    flux = lax.dot_general(
        w_out_ref[...], second, (((1,), (1,)), ((), ())), preferred_element_type=jnp.float32
    )

    tile = tile_ref[...]
    named = (tile == lax.broadcasted_iota(jnp.int32, (count, cells), 0)).astype(jnp.float32)
    ahead = (
        lax.broadcasted_iota(jnp.int32, (cells, cells), 0)
        < lax.broadcasted_iota(jnp.int32, (cells, cells), 1)
    ).astype(jnp.float32)
    rank = jnp.dot(
        named.astype(jnp.bfloat16), ahead.astype(jnp.bfloat16), preferred_element_type=jnp.float32
    )
    slot = jnp.sum(rank * named, axis=0, keepdims=True).astype(jnp.int32)
    key = tile * cap + slot
    spot = spot_ref[...]
    spots = jnp.where(
        lax.broadcasted_iota(jnp.int32, (16, cells), 0) == 0, spot // LANES, spot % LANES
    ).astype(jnp.float32)
    high = flux.astype(jnp.bfloat16)
    low = (flux - high.astype(jnp.float32)).astype(jnp.bfloat16)
    parts = jnp.concatenate([high, low, spots.astype(jnp.bfloat16)], axis=0)
    lane_of = lax.broadcasted_iota(jnp.int32, (LANES, cells), 0)

    @pl.loop(0, blocks)
    def _(j):
        taken = (key - j * LANES == lane_of).astype(jnp.float32).astype(jnp.bfloat16)
        placed = lax.dot_general(
            parts, taken, (((1,), (1,)), ((), ())), preferred_element_type=jnp.float32
        )
        summed = placed[0:tr] + placed[tr : 2 * tr]
        slots[0, j] = summed[0:8]
        slots[1, j] = summed[8:16]
        slots[2, j] = placed[2 * tr : 2 * tr + 8]

    stacked = [slots[h].reshape(8 * blocks, LANES) for h in range(3)]
    laneb = lax.broadcasted_iota(jnp.int32, (8 * blocks, LANES), 1)
    for g in range(groups):
        turned = [
            pltpu.roll(s, (cap * (h - g)) % LANES, 1) if h != g else s
            for h, s in enumerate(stacked)
        ]
        packed = jnp.where(laneb < cap, turned[0], jnp.where(laneb < 2 * cap, turned[1], turned[2]))
        route_out[blocks * g : blocks * (g + 1)] = packed.reshape(blocks, 8, LANES)

    pl.semaphore_wait(barrier, count - 1)

    def route_copy(d, origin):
        return pltpu.make_async_remote_copy(
            src_ref=route_out.at[place(d)],
            dst_ref=route_in.at[place(origin)],
            send_sem=route_send.at[d],
            recv_sem=route_recv.at[origin],
            device_id=(d // n_lon, lax.rem(d, n_lon)),
            device_id_type=MESH,
        )

    @pl.loop(1, count)
    def _(o):
        route_copy(lax.rem(me + o, count), me).start()

    route_in[place(me)] = route_out[place(me)]

    @pl.loop(1, count)
    def _(o):
        route_copy(me, lax.rem(me + o, count)).wait_recv()

    lists = [jnp.zeros((8 * blocks, LANES), jnp.float32)] * 3
    for g in range(groups):
        got = route_in[blocks * g : blocks * (g + 1)].reshape(8 * blocks, LANES)
        for h in range(3):
            turned = pltpu.roll(got, (cap * (g - h)) % LANES, 1) if g != h else got
            lists[h] = jnp.where(laneb // cap == g, turned, lists[h])
    entries = [
        jnp.concatenate([part[8 * j : 8 * (j + 1)] for j in range(blocks)], axis=1)
        for part in lists
    ]
    values = jnp.concatenate(entries[:2], axis=0)
    at_row, at_lane = entries[2][0:1], entries[2][1:2]
    wide = blocks * LANES
    onto = (
        lax.broadcasted_iota(jnp.int32, (LANES, wide), 0).astype(jnp.float32) == at_lane
    ).astype(jnp.float32)
    spread = jnp.concatenate(
        [jnp.where(at_row == float(a), values, 0.0) for a in range(rows)], axis=0
    )
    high = spread.astype(jnp.bfloat16)
    low = (spread - high.astype(jnp.float32)).astype(jnp.bfloat16)
    emitted = lax.dot_general(
        jnp.concatenate([high, low], axis=0),
        onto.astype(jnp.bfloat16),
        (((1,), (1,)), ((), ())),
        preferred_element_type=jnp.float32,
    )
    emitted = emitted[: rows * tr] + emitted[rows * tr :]

    out_ref[...] = emitted

    @pl.loop(1, count)
    def _(o):
        route_copy(lax.rem(me + o, count), me).wait_send()


def zonal_kernel(
    n_lon,
    x_ref,
    zon_ref,
    emitted_ref,
    st,
    lon_out,
    lon_in,
    gz,
    gze,
    held,
    lon_sem,
):
    lev, rows, _ = zon_ref.shape
    tr = st.shape[2]
    per = lev * rows
    lat, lon = lax.axis_index("lat"), lax.axis_index("lon")
    west, east = lax.rem(lon + n_lon - 1, n_lon), lax.rem(lon + 1, n_lon)
    barrier = pltpu.get_barrier_semaphore()
    for side in (west, east):
        pl.semaphore_signal(barrier, inc=1, device_id=(lat, side), device_id_type=MESH)

    lane = lax.broadcasted_iota(jnp.int32, (tr, LANES), 1)
    lane8 = lax.broadcasted_iota(jnp.int32, (rows, LANES), 1)

    def column(k, a):
        return x_ref[pl.ds(k * rows + a, tr, stride=per), :]

    @pl.loop(0, lev // 2)
    def _(kp):
        left = jnp.zeros((tr, LANES), jnp.float32)
        right = left
        for p in range(2 * rows):
            q = column(2 * kp + p // rows, p % rows)
            if p < rows:
                q = q + jnp.where(kp == 0, emitted_ref[p * tr : (p + 1) * tr], 0.0)
            held[2 * kp + p // rows, p % rows] = q
            mine = lane // 8 == p
            left = jnp.where(mine, pltpu.roll(q, 8 * p, 1), left)
            right = jnp.where(mine, pltpu.roll(q, (8 * p + 8) % LANES, 1), right)
        lon_out[0, pl.ds(2 * kp, 2)] = left.reshape(2, 8, LANES)
        lon_out[1, pl.ds(2 * kp, 2)] = right.reshape(2, 8, LANES)

    left = jnp.zeros((rows, LANES), jnp.float32)
    right = left
    for k in range(lev):
        c = zon_ref[k]
        mine = lane8 // 8 == k
        left = jnp.where(mine, pltpu.roll(c, (8 * k) % LANES, 1), left)
        right = jnp.where(mine, pltpu.roll(c, (8 * k + 8) % LANES, 1), right)
    lon_out[0, lev] = left
    lon_out[1, lev] = right

    pl.semaphore_wait(barrier, 2)

    def lon_copy(side):
        return pltpu.make_async_remote_copy(
            src_ref=lon_out.at[side],
            dst_ref=lon_in.at[side],
            send_sem=lon_sem.at[0, side],
            recv_sem=lon_sem.at[1, side],
            device_id=(lat, (west, east)[side]),
            device_id_type=MESH,
        )

    lon_copy(0).start()
    lon_copy(1).start()
    lon_copy(0).wait_recv()
    lon_copy(1).wait_recv()

    def ring(main, ext, m, where):
        if m == 0:
            return main, ext
        if m > 0:
            mask, turn = where < m, LANES - m
        else:
            mask, turn = where >= LANES + m, -m
        return (
            pltpu.roll(jnp.where(mask, ext, main), turn, 1),
            pltpu.roll(jnp.where(mask, main, ext), turn, 1),
        )

    def unpack(from_west, from_east, p, where):
        return jnp.where(
            where < 8,
            pltpu.roll(from_east, (LANES - 8 * p) % LANES, 1),
            pltpu.roll(from_west, (LANES - 8 - 8 * p) % LANES, 1),
        )

    @pl.loop(0, lev)
    def _(k):
        c = zon_ref[k]
        ce = jnp.where(
            lane8 < 8,
            pltpu.roll(lon_in[0, lev], lax.rem(LANES - 8 * k, LANES), 1),
            pltpu.roll(lon_in[1, lev], LANES - 8 - 8 * k, 1),
        )
        before, before_e = ring(c, ce, -1, lane8)
        for m, weight in enumerate(cell_weights(c, before)):
            gz[k, m] = weight
        for m, weight in enumerate(cell_weights(ce, before_e)):
            gze[k, m] = weight

    def zonal(k, a, main, ext):
        new, new_e = 0.0, 0.0
        for m in range(-3, 4):
            near, near_e = ring(main, ext, m, lane)
            new = new + near * gz[k, m + 3, a : a + 1, :]
            new_e = new_e + near_e * gze[k, m + 3, a : a + 1, :]
        main, ext = new, new_e
        new = 0.0
        for m in range(-3, 4):
            if m == 0:
                near = main
            elif m > 0:
                near = pltpu.roll(jnp.where(lane < m, ext, main), LANES - m, 1)
            else:
                near = pltpu.roll(jnp.where(lane >= LANES + m, ext, main), -m, 1)
            new = new + near * gz[k, m + 3, a : a + 1, :]
        st[k, a] = new

    def pair(kp, parities):
        from_west = lon_in[1, pl.ds(2 * kp, 2)].reshape(tr, LANES)
        from_east = lon_in[0, pl.ds(2 * kp, 2)].reshape(tr, LANES)
        for parity in parities:
            k = 2 * kp + parity
            for a in range(rows):
                ext = unpack(from_west, from_east, parity * rows + a, lane)
                zonal(k, a, held[k, a], ext)

    @pl.loop(0, lev // 2)
    def _(kp):
        pair(kp, (0, 1))

    lon_copy(0).wait_send()
    lon_copy(1).wait_send()


def meridional_kernel(
    n_lat,
    st,
    mer_ref,
    fin,
    mer_in,
    halo,
    gm,
    mer_sem,
    lat_send,
    lat_recv,
):
    lev, rows, tr, _ = st.shape
    lat, lon = lax.axis_index("lat"), lax.axis_index("lon")
    has_south, has_north = lat > 0, lat < n_lat - 1
    barrier = pltpu.get_barrier_semaphore()

    @pl.when(has_south)
    def _():
        pl.semaphore_signal(barrier, inc=1, device_id=(lat - 1, lon), device_id_type=MESH)

    @pl.when(has_north)
    def _():
        pl.semaphore_signal(barrier, inc=1, device_id=(lat + 1, lon), device_id_type=MESH)

    between = jnp.logical_and(has_south, has_north)

    @pl.when(between)
    def _():
        pl.semaphore_wait(barrier, 2)

    @pl.when(jnp.logical_not(between))
    def _():
        pl.semaphore_wait(barrier, 1)

    def mer_copy(side):
        return pltpu.make_async_remote_copy(
            src_ref=mer_ref,
            dst_ref=mer_in.at[side],
            send_sem=mer_sem.at[0, side],
            recv_sem=mer_sem.at[1, side],
            device_id=(lat + (-1, 1)[side], lon),
            device_id_type=MESH,
        )

    def lat_copy(k, side):
        return pltpu.make_async_remote_copy(
            src_ref=st.at[k, pl.ds((0, rows - WIDE)[side], WIDE)],
            dst_ref=halo.at[side, k],
            send_sem=lat_send.at[side, k],
            recv_sem=lat_recv.at[side, k],
            device_id=(lat + (-1, 1)[side], lon),
            device_id_type=MESH,
        )

    @pl.when(has_south)
    def _():
        mer_copy(0).start()

    @pl.when(has_north)
    def _():
        mer_copy(1).start()

    @pl.loop(0, lev)
    def _(k):
        @pl.when(has_south)
        def _():
            lat_copy(k, 0).start()

        @pl.when(has_north)
        def _():
            lat_copy(k, 1).start()

    @pl.when(jnp.logical_not(has_south))
    def _():
        mer_in[1] = jnp.zeros((lev, rows, LANES), jnp.float32)

        @pl.loop(0, lev)
        def _(k):
            halo[1, k] = jnp.zeros((WIDE, tr, LANES), jnp.float32)

    @pl.when(jnp.logical_not(has_north))
    def _():
        mer_in[0] = jnp.zeros((lev, rows, LANES), jnp.float32)

        @pl.loop(0, lev)
        def _(k):
            halo[0, k] = jnp.zeros((WIDE, tr, LANES), jnp.float32)

    @pl.when(has_south)
    def _():
        mer_copy(1).wait_recv()

    @pl.when(has_north)
    def _():
        mer_copy(0).wait_recv()

    grid_row = lax.broadcasted_iota(jnp.int32, (3 * rows, LANES), 0) + (lat - 1) * rows
    northern = (grid_row < n_lat * rows - 1).astype(jnp.float32)

    @pl.loop(0, lev)
    def _(k):
        c = jnp.concatenate([mer_in[1, k], mer_ref[k], mer_in[0, k]], axis=0) * northern
        for m, weight in enumerate(cell_weights(c, pltpu.roll(c, 1, 0))):
            gm[k, m] = weight

    def meridional(k):
        @pl.when(has_south)
        def _():
            lat_copy(k, 1).wait_recv()

        @pl.when(has_north)
        def _():
            lat_copy(k, 0).wait_recv()

        whole = (
            [halo[1, k, a] for a in range(WIDE)]
            + [st[k, a] for a in range(rows)]
            + [halo[0, k, a] for a in range(WIDE)]
        )
        once = []
        for a in range(-3, rows + 3):
            new = 0.0
            for m in range(7):
                new = new + whole[a + 3 + m] * gm[k, m, a + rows : a + rows + 1]
            once.append(new)
        for a in range(rows):
            new = 0.0
            for m in range(7):
                new = new + once[a + m] * gm[k, m, a + rows : a + rows + 1]
            fin[k, a] = new

    @pl.loop(0, lev)
    def _(k):
        meridional(k)

    @pl.when(has_south)
    def _():
        mer_copy(0).wait_send()

        @pl.loop(0, lev)
        def _(k):
            lat_copy(k, 0).wait_send()

    @pl.when(has_north)
    def _():
        mer_copy(1).wait_send()

        @pl.loop(0, lev)
        def _(k):
            lat_copy(k, 1).wait_send()


def mixing_kernel(fin, mix_ref, out_ref):
    lev, rows, tr, _ = fin.shape
    per = lev * rows

    @pl.loop(0, rows)
    def _(a):
        part = [fin[j, a] for j in range(lev)]
        for k in range(lev):
            total = part[0] * mix_ref[a, k, 0]
            for j in range(1, lev):
                total = total + part[j] * mix_ref[a, k, j]
            out_ref[pl.ds(k * rows + a, tr, stride=per), :] = total


def on_device(
    n_lat,
    n_lon,
    features,
    land_tile,
    land_spot,
    w_in,
    b_in,
    w_mid,
    b_mid,
    w_out,
    tracers,
    zonal_wind,
    meridional_wind,
    mixing,
):
    tr, lev, rows, cols = tracers.shape
    cells = features.shape[0]
    count = n_lat * n_lon
    cap = 2 * cells // count
    f32 = jnp.float32
    vmem = pl.BlockSpec(memory_space=pltpu.VMEM)
    smem = pl.BlockSpec(memory_space=pltpu.SMEM)
    dma = pltpu.SemaphoreType.DMA

    def params(number):
        return pltpu.CompilerParams(
            collective_id=number, has_side_effects=True, vmem_limit_bytes=16 * 1024 * 1024
        )

    emitted = pl.pallas_call(
        functools.partial(route_kernel, n_lat, n_lon, cap, tr, rows),
        out_shape=jax.ShapeDtypeStruct((rows * tr, cols), f32),
        in_specs=[vmem] * 8,
        out_specs=vmem,
        scratch_shapes=[
            pltpu.VMEM((count, 8, cols), f32),
            pltpu.VMEM((count, 8, cols), f32),
            pltpu.VMEM((3, count * cap // cols, 8, cols), f32),
            dma((count,)),
            dma((count,)),
        ],
        compiler_params=params(0),
    )(
        features.T,
        land_tile.T,
        land_spot.reshape(1, -1),
        w_in,
        b_in.reshape(1, -1),
        w_mid,
        b_mid.reshape(1, -1),
        w_out.T,
    )
    blown = pl.pallas_call(
        functools.partial(zonal_kernel, n_lon),
        out_shape=jax.ShapeDtypeStruct((lev, rows, tr, cols), f32),
        in_specs=[vmem] * 3,
        out_specs=vmem,
        scratch_shapes=[
            pltpu.VMEM((2, lev + 1, 8, cols), f32),
            pltpu.VMEM((2, lev + 1, 8, cols), f32),
            pltpu.VMEM((lev, 7, rows, cols), f32),
            pltpu.VMEM((lev, 7, rows, cols), f32),
            pltpu.VMEM((lev, rows, tr, cols), f32),
            dma((2, 2)),
        ],
        compiler_params=params(1),
    )(tracers.reshape(tr * lev * rows, cols), zonal_wind, emitted)
    swept = pl.pallas_call(
        functools.partial(meridional_kernel, n_lat),
        out_shape=jax.ShapeDtypeStruct((lev, rows, tr, cols), f32),
        in_specs=[vmem] * 2,
        out_specs=vmem,
        scratch_shapes=[
            pltpu.VMEM((2, lev, rows, cols), f32),
            pltpu.VMEM((2, lev, WIDE, tr, cols), f32),
            pltpu.VMEM((lev, 7, 3 * rows, cols), f32),
            dma((2, 2)),
            dma((2, lev)),
            dma((2, lev)),
        ],
        compiler_params=params(2),
    )(blown, meridional_wind)
    out = pl.pallas_call(
        mixing_kernel,
        out_shape=jax.ShapeDtypeStruct((tr * lev * rows, cols), f32),
        in_specs=[vmem, smem],
        out_specs=vmem,
        compiler_params=pltpu.CompilerParams(vmem_limit_bytes=16 * 1024 * 1024),
    )(swept, mixing)
    return out.reshape(tr, lev, rows, cols)


def solution(mesh):
    placed = (
        P(("lat", "lon"), None),
        P(("lat", "lon"), None),
        P(("lat", "lon")),
        P(),
        P(),
        P(),
        P(),
        P(),
        P(None, None, "lat", "lon"),
        P(None, "lat", "lon"),
        P(None, "lat", "lon"),
        P("lat", None, None),
    )
    return jax.shard_map(
        functools.partial(on_device, mesh.shape["lat"], mesh.shape["lon"]),
        mesh=mesh,
        in_specs=placed,
        out_specs=P(None, None, "lat", "lon"),
        check_vma=False,
    )
```

```python
import functools

import jax
import jax.numpy as jnp
from jax import lax
from jax.experimental import pallas as pl
from jax.experimental.pallas import tpu as pltpu
from jax.sharding import PartitionSpec as P

MESH = pl.DeviceIdType.MESH
LANES = 128
WIDE = 6


def silu(v):
    return v / (1.0 + jnp.exp(-v))


def face_weights(c):
    p = jnp.maximum(c, 0.0)
    w = jnp.maximum(-c, 0.0)
    alpha = 0.5 * p * p
    beta = 1.0 - 2.0 / 3.0 * p
    gamma = 0.5 * w * w
    delta = 1.0 - 2.0 / 3.0 * w
    x = alpha * (1.0 - 3.0 * beta)
    y = c - alpha * (1.0 + 3.0 * beta) + gamma * (1.0 + 3.0 * delta)
    z = -gamma * (1.0 - 3.0 * delta)
    u = 6.0 * alpha * beta
    v = -6.0 * gamma * delta
    a, b = 7.0 / 12.0, 1.0 / 12.0
    return [
        -b * x,
        a * x - b * y,
        a * (x + y) - b * z + u,
        a * (y + z) - b * x + v,
        a * z - b * y,
        -b * z,
    ]


def cell_weights(c, before):
    f, g = face_weights(c), face_weights(before)
    out = [g[0]]
    for m in range(5):
        out.append(g[m + 1] - f[m])
    out.append(-f[5])
    out[3] = out[3] + 1.0
    return out


def kernel(
    n_lat,
    n_lon,
    cap,
    *refs,
):
    given, refs = refs[:12], refs[12:]
    out_ref, held, refs = refs[0], refs[1:13], refs[13:]
    transport_step(n_lat, n_lon, cap, given, held, out_ref, *refs)


def transport_step(
    n_lat,
    n_lon,
    cap,
    given,
    held,
    out_ref,
    given_sem,
    zb,
    once_z,
    twice_z,
    wz,
    wk,
    mer_in,
    route_out,
    route_in,
    gm,
    st,
    fin,
    acc,
    slots,
    lon_sem,
    lon0_sem,
    mer_sem,
    route_send,
    route_recv,
    lat_send,
    lat_recv,
):
    (
        feat_ref,
        tile_ref,
        spot_ref,
        w_in_ref,
        b_in_ref,
        w_mid_ref,
        b_mid_ref,
        w_out_ref,
        x_ref,
        zon_ref,
        mer_ref,
        mix_ref,
    ) = held
    lev, rows, _ = zon_ref.shape
    cells = feat_ref.shape[1]
    tr = st.shape[2]
    per = lev * rows
    count = n_lat * n_lon
    groups = LANES // cap
    blocks = count // groups
    lat, lon = lax.axis_index("lat"), lax.axis_index("lon")
    me = lat * n_lon + lon
    west, east = lax.rem(lon + n_lon - 1, n_lon), lax.rem(lon + 1, n_lon)
    has_south, has_north = lat > 0, lat < n_lat - 1

    def place(d):
        return lax.rem(d, groups) * blocks + d // groups

    def load(i):
        return pltpu.make_async_copy(given[i], held[i], given_sem.at[i])

    for i in (8, 9, 10, 0, 3, 5, 4, 6, 7, 1, 2, 11):
        load(i).start()

    barrier = pltpu.get_barrier_semaphore()

    @pl.loop(1, count)
    def _(o):
        d = lax.rem(me + o, count)
        pl.semaphore_signal(
            barrier, inc=1, device_id=(d // n_lon, lax.rem(d, n_lon)), device_id_type=MESH
        )

    @pl.when(jnp.logical_not(has_south))
    def _():
        mer_in[1] = jnp.zeros((lev, rows, LANES), jnp.float32)

        @pl.loop(0, lev)
        def _(k):
            st[k, 0:WIDE] = jnp.zeros((WIDE, tr, LANES), jnp.float32)

    @pl.when(jnp.logical_not(has_north))
    def _():
        mer_in[0] = jnp.zeros((lev, rows, LANES), jnp.float32)

        @pl.loop(0, lev)
        def _(k):
            st[k, WIDE + rows :] = jnp.zeros((WIDE, tr, LANES), jnp.float32)

    load(8).wait()

    def halves(v):
        high = v.astype(jnp.bfloat16)
        low = (v - high.astype(jnp.float32)).astype(jnp.bfloat16)
        return jnp.concatenate([high, low], axis=1)

    def turned_by(order, v):
        return lax.dot_general(
            order, halves(v), (((1,), (1,)), ((), ())), preferred_element_type=jnp.float32
        )

    cell = lax.broadcasted_iota(jnp.int32, (LANES, 2 * LANES), 0)
    from_cell = lax.broadcasted_iota(jnp.int32, (LANES, 2 * LANES), 1) % LANES
    straight = (cell == from_cell).astype(jnp.float32).astype(jnp.bfloat16)
    by_row = (cell % tr * rows + cell // tr == from_cell).astype(jnp.float32).astype(jnp.bfloat16)
    own = slice(16, 16 + LANES)

    @pl.loop(1, lev)
    def _(k):
        zb[k, own] = turned_by(straight, x_ref[:, k].reshape(tr * rows, LANES))

    load(9).wait()
    zb[lev, own] = turned_by(straight, zon_ref[...].reshape(lev * rows, LANES))

    pl.semaphore_wait(barrier, count - 1)

    def lon_copy(side):
        return pltpu.make_async_remote_copy(
            src_ref=zb.at[pl.ds(1, lev), pl.ds((16, 8 + LANES)[side], 8)],
            dst_ref=zb.at[pl.ds(1, lev), pl.ds((16 + LANES, 8)[side], 8)],
            send_sem=lon_sem.at[0, side],
            recv_sem=lon_sem.at[1, side],
            device_id=(lat, (west, east)[side]),
            device_id_type=MESH,
        )

    def lon0_copy(side):
        return pltpu.make_async_remote_copy(
            src_ref=zb.at[0, pl.ds((16, 8 + LANES)[side], 8)],
            dst_ref=zb.at[0, pl.ds((16 + LANES, 8)[side], 8)],
            send_sem=lon0_sem.at[0, side],
            recv_sem=lon0_sem.at[1, side],
            device_id=(lat, (west, east)[side]),
            device_id_type=MESH,
        )

    def mer_copy(side):
        return pltpu.make_async_remote_copy(
            src_ref=mer_ref,
            dst_ref=mer_in.at[side],
            send_sem=mer_sem.at[0, side],
            recv_sem=mer_sem.at[1, side],
            device_id=(lat + (-1, 1)[side], lon),
            device_id_type=MESH,
        )

    def lat_copy(k, side):
        return pltpu.make_async_remote_copy(
            src_ref=st.at[k, pl.ds((WIDE, rows)[side], WIDE)],
            dst_ref=st.at[k, pl.ds((WIDE + rows, 0)[side], WIDE)],
            send_sem=lat_send.at[side, k],
            recv_sem=lat_recv.at[side, k],
            device_id=(lat + (-1, 1)[side], lon),
            device_id_type=MESH,
        )

    def route_copy(d, origin):
        return pltpu.make_async_remote_copy(
            src_ref=route_out.at[place(d)],
            dst_ref=route_in.at[place(origin)],
            send_sem=route_send.at[d],
            recv_sem=route_recv.at[origin],
            device_id=(d // n_lon, lax.rem(d, n_lon)),
            device_id_type=MESH,
        )

    lon_copy(0).start()
    lon_copy(1).start()
    load(10).wait()

    @pl.when(has_south)
    def _():
        mer_copy(0).start()

    @pl.when(has_north)
    def _():
        mer_copy(1).start()

    for i in (0, 3, 5, 4, 6, 7, 1, 2):
        load(i).wait()
    first = silu(
        lax.dot_general(
            feat_ref[...], w_in_ref[...], (((0,), (0,)), ((), ())), preferred_element_type=jnp.float32
        )
        + b_in_ref[...]
    ).astype(jnp.bfloat16)
    second = silu(
        jnp.dot(first, w_mid_ref[...], preferred_element_type=jnp.float32) + b_mid_ref[...]
    ).astype(jnp.bfloat16)
    flux = lax.dot_general(
        w_out_ref[...], second, (((1,), (1,)), ((), ())), preferred_element_type=jnp.float32
    )

    lon_copy(0).wait_recv()
    lon_copy(1).wait_recv()

    wide_cols = LANES + 16
    c = zb[lev, 8 : 8 + wide_cols]
    before = zb[lev, 7 : 7 + wide_cols]
    for m, weight in enumerate(cell_weights(c, before)):
        wz[m * wide_cols : (m + 1) * wide_cols] = halves(weight)
    pick_from = lax.broadcasted_iota(jnp.int32, (2 * LANES, LANES), 0) % LANES
    pick_row = lax.broadcasted_iota(jnp.int32, (2 * LANES, LANES), 1) % rows

    def zonal(k):
        pick = (pick_from == pick_row + k * rows).astype(jnp.float32).astype(jnp.bfloat16)
        for m in range(7):
            wk[m * wide_cols : (m + 1) * wide_cols] = jnp.dot(
                wz[m * wide_cols : (m + 1) * wide_cols], pick, preferred_element_type=jnp.float32
            )
        third = wide_cols // 3

        @pl.loop(0, 3)
        def _(i):
            new = 0.0
            for m in range(7):
                new = new + (
                    zb[k, pl.ds(i * third + 5 + m, third)]
                    * wk[pl.ds(pl.multiple_of(i * third + m * wide_cols, 8), third)]
                )
            once_z[pl.ds(pl.multiple_of(i * third + 8, 8), third)] = new

        half = LANES // 2

        @pl.loop(0, 2)
        def _(i):
            new = 0.0
            for m in range(7):
                new = new + (
                    once_z[pl.ds(i * half + 13 + m, half)]
                    * wk[pl.ds(pl.multiple_of(i * half + 8 + m * wide_cols, 8), half)]
                )
            twice_z[pl.ds(pl.multiple_of(i * half, 8), half)] = new

        st[k, WIDE : WIDE + rows] = turned_by(by_row, twice_z[...]).reshape(rows, tr, LANES)

    def send_rows(k):
        @pl.when(has_south)
        def _():
            lat_copy(k, 0).start()

        @pl.when(has_north)
        def _():
            lat_copy(k, 1).start()

    @pl.loop(1, lev // 2)
    def _(k):
        zonal(k)
        send_rows(k)

    tile = tile_ref[...]
    named = (tile == lax.broadcasted_iota(jnp.int32, (count, cells), 0)).astype(jnp.float32)
    ahead = (
        lax.broadcasted_iota(jnp.int32, (cells, cells), 0)
        < lax.broadcasted_iota(jnp.int32, (cells, cells), 1)
    ).astype(jnp.float32)
    rank = jnp.dot(
        named.astype(jnp.bfloat16), ahead.astype(jnp.bfloat16), preferred_element_type=jnp.float32
    )
    slot = jnp.sum(rank * named, axis=0, keepdims=True).astype(jnp.int32)
    key = tile * cap + slot
    spot = spot_ref[...]
    spots = jnp.where(
        lax.broadcasted_iota(jnp.int32, (16, cells), 0) == 0, spot // LANES, spot % LANES
    ).astype(jnp.float32)
    high = flux.astype(jnp.bfloat16)
    low = (flux - high.astype(jnp.float32)).astype(jnp.bfloat16)
    parts = jnp.concatenate([high, low, spots.astype(jnp.bfloat16)], axis=0)
    lane_of = lax.broadcasted_iota(jnp.int32, (LANES, cells), 0)

    @pl.loop(0, blocks)
    def _(j):
        taken = (key - j * LANES == lane_of).astype(jnp.float32).astype(jnp.bfloat16)
        placed = lax.dot_general(
            parts, taken, (((1,), (1,)), ((), ())), preferred_element_type=jnp.float32
        )
        summed = placed[0:tr] + placed[tr : 2 * tr]
        slots[0, j] = summed[0:8]
        slots[1, j] = summed[8:16]
        slots[2, j] = placed[2 * tr : 2 * tr + 8]

    stacked = [slots[h].reshape(8 * blocks, LANES) for h in range(3)]
    laneb = lax.broadcasted_iota(jnp.int32, (8 * blocks, LANES), 1)
    for g in range(groups):
        turned = [
            pltpu.roll(s, (cap * (h - g)) % LANES, 1) if h != g else s
            for h, s in enumerate(stacked)
        ]
        packed = jnp.where(laneb < cap, turned[0], jnp.where(laneb < 2 * cap, turned[1], turned[2]))
        route_out[blocks * g : blocks * (g + 1)] = packed.reshape(blocks, 8, LANES)

    @pl.loop(1, count)
    def _(o):
        route_copy(lax.rem(me + o, count), me).start()

    route_in[place(me)] = route_out[place(me)]

    @pl.loop(lev // 2, lev)
    def _(k):
        zonal(k)
        send_rows(k)

    @pl.when(has_south)
    def _():
        mer_copy(1).wait_recv()

    @pl.when(has_north)
    def _():
        mer_copy(0).wait_recv()

    grid_row = lax.broadcasted_iota(jnp.int32, (3 * rows, LANES), 0) + (lat - 1) * rows
    northern = (grid_row < n_lat * rows - 1).astype(jnp.float32)

    @pl.loop(0, lev)
    def _(k):
        c = jnp.concatenate([mer_in[1, k], mer_ref[k], mer_in[0, k]], axis=0) * northern
        for m, weight in enumerate(cell_weights(c, pltpu.roll(c, 1, 0))):
            gm[k, m] = weight

    @pl.loop(1, count)
    def _(o):
        route_copy(me, lax.rem(me + o, count)).wait_recv()

    lists = [jnp.zeros((8 * blocks, LANES), jnp.float32)] * 3
    for g in range(groups):
        got = route_in[blocks * g : blocks * (g + 1)].reshape(8 * blocks, LANES)
        for h in range(3):
            turned = pltpu.roll(got, (cap * (g - h)) % LANES, 1) if g != h else got
            lists[h] = jnp.where(laneb // cap == g, turned, lists[h])
    entries = [
        jnp.concatenate([part[8 * j : 8 * (j + 1)] for j in range(blocks)], axis=1)
        for part in lists
    ]
    values = jnp.concatenate(entries[:2], axis=0)
    at_row, at_lane = entries[2][0:1], entries[2][1:2]
    wide = blocks * LANES
    onto = (
        lax.broadcasted_iota(jnp.int32, (LANES, wide), 0).astype(jnp.float32) == at_lane
    ).astype(jnp.float32)
    row_of = lax.broadcasted_iota(jnp.int32, (rows, wide), 0).astype(jnp.float32)
    spread = jnp.concatenate(
        [jnp.where(at_row == row_of, values[t : t + 1], 0.0) for t in range(tr)], axis=0
    )
    high = spread.astype(jnp.bfloat16)
    low = (spread - high.astype(jnp.float32)).astype(jnp.bfloat16)
    emitted = lax.dot_general(
        jnp.concatenate([high, low], axis=0),
        onto.astype(jnp.bfloat16),
        (((1,), (1,)), ((), ())),
        preferred_element_type=jnp.float32,
    )
    emitted = emitted[: rows * tr] + emitted[rows * tr :]

    surface = x_ref[:, 0].reshape(tr * rows, LANES) + emitted
    zb[0, own] = turned_by(straight, surface)
    lon0_copy(0).start()
    lon0_copy(1).start()

    def meridional(k):
        @pl.when(has_south)
        def _():
            lat_copy(k, 1).wait_recv()

        @pl.when(has_north)
        def _():
            lat_copy(k, 0).wait_recv()

        once = []
        for a in range(-3, rows + 3):
            new = 0.0
            for m in range(7):
                new = new + st[k, a + 3 + m] * gm[k, m, a + rows : a + rows + 1]
            once.append(new)
        for a in range(rows):
            new = 0.0
            for m in range(7):
                new = new + once[a + m] * gm[k, m, a + rows : a + rows + 1]
            fin[k, a] = new

    def mixed(levels, opening, closing):
        @pl.loop(0, rows)
        def _(a):
            part = [fin[j, a] for j in levels]
            for k in range(lev):
                total = 0.0 if opening else acc[a, k]
                for j, value in zip(levels, part):
                    total = total + value * mix_ref[a, k, j]
                if closing:
                    out_ref[pl.ds(k * rows + a, tr, stride=per), :] = total
                else:
                    acc[a, k] = total

    cuts = [1, 1 + lev // 3, 1 + 2 * (lev // 3), lev]

    def some(i):
        @pl.loop(cuts[i], cuts[i + 1])
        def _(k):
            meridional(k)

        mixed(range(cuts[i], cuts[i + 1]), i == 0, False)

    load(11).wait()
    some(0)
    lon0_copy(0).wait_recv()
    lon0_copy(1).wait_recv()
    zonal(0)
    send_rows(0)
    some(1)
    some(2)
    meridional(0)
    mixed(range(1), False, True)

    for side in range(2):
        lon_copy(side).wait_send()
        lon0_copy(side).wait_send()

    @pl.loop(1, count)
    def _(o):
        route_copy(lax.rem(me + o, count), me).wait_send()

    @pl.when(has_south)
    def _():
        mer_copy(0).wait_send()

        @pl.loop(0, lev)
        def _(k):
            lat_copy(k, 0).wait_send()

    @pl.when(has_north)
    def _():
        mer_copy(1).wait_send()

        @pl.loop(0, lev)
        def _(k):
            lat_copy(k, 1).wait_send()


def on_device(
    n_lat,
    n_lon,
    features,
    land_tile,
    land_spot,
    w_in,
    b_in,
    w_mid,
    b_mid,
    w_out,
    tracers,
    zonal_wind,
    meridional_wind,
    mixing,
):
    tr, lev, rows, cols = tracers.shape
    cells = features.shape[0]
    count = n_lat * n_lon
    cap = 2 * cells // count
    f32 = jnp.float32
    args = (
        features.T,
        land_tile.T,
        land_spot.reshape(1, -1),
        w_in,
        b_in.reshape(1, -1),
        w_mid,
        b_mid.reshape(1, -1),
        w_out.T,
        tracers,
        zonal_wind,
        meridional_wind,
        mixing,
    )
    out = pl.pallas_call(
        functools.partial(kernel, n_lat, n_lon, cap),
        out_shape=jax.ShapeDtypeStruct((tr * lev * rows, cols), f32),
        in_specs=[pl.BlockSpec(memory_space=pltpu.HBM)] * len(args),
        out_specs=pl.BlockSpec(memory_space=pltpu.VMEM),
        scratch_shapes=[pltpu.VMEM(arg.shape, arg.dtype) for arg in args[:-1]]
        + [
            pltpu.SMEM(mixing.shape, f32),
            pltpu.SemaphoreType.DMA((len(args),)),
            pltpu.VMEM((lev + 1, cols + 32, tr * rows), f32),
            pltpu.VMEM((cols + 32, tr * rows), f32),
            pltpu.VMEM((cols, tr * rows), f32),
            pltpu.VMEM((7 * (cols + 16), 2 * lev * rows), jnp.bfloat16),
            pltpu.VMEM((7 * (cols + 16), tr * rows), f32),
            pltpu.VMEM((2, lev, rows, cols), f32),
            pltpu.VMEM((count, 8, cols), f32),
            pltpu.VMEM((count, 8, cols), f32),
            pltpu.VMEM((lev, 7, 3 * rows, cols), f32),
            pltpu.VMEM((lev, rows + 2 * WIDE, tr, cols), f32),
            pltpu.VMEM((lev, rows, tr, cols), f32),
            pltpu.VMEM((rows, lev, tr, cols), f32),
            pltpu.VMEM((3, count * cap // cols, 8, cols), f32),
            pltpu.SemaphoreType.DMA((2, 2)),
            pltpu.SemaphoreType.DMA((2, 2)),
            pltpu.SemaphoreType.DMA((2, 2)),
            pltpu.SemaphoreType.DMA((count,)),
            pltpu.SemaphoreType.DMA((count,)),
            pltpu.SemaphoreType.DMA((2, lev)),
            pltpu.SemaphoreType.DMA((2, lev)),
        ],
        compiler_params=pltpu.CompilerParams(
            collective_id=0, has_side_effects=True, vmem_limit_bytes=60 * 1024 * 1024
        ),
    )(*args)
    return out.reshape(tr, lev, rows, cols)


def solution(mesh):
    placed = (
        P(("lat", "lon"), None),
        P(("lat", "lon"), None),
        P(("lat", "lon")),
        P(),
        P(),
        P(),
        P(),
        P(),
        P(None, None, "lat", "lon"),
        P(None, "lat", "lon"),
        P(None, "lat", "lon"),
        P("lat", None, None),
    )
    return jax.shard_map(
        functools.partial(on_device, mesh.shape["lat"], mesh.shape["lon"]),
        mesh=mesh,
        in_specs=placed,
        out_specs=P(None, None, "lat", "lon"),
        check_vma=False,
    )
```

```python
import functools

import jax
import jax.numpy as jnp
from jax import lax
from jax.experimental import pallas as pl
from jax.experimental.pallas import tpu as pltpu
from jax.sharding import PartitionSpec as P

MESH = pl.DeviceIdType.MESH
LANES = 128
WIDE = 6


def silu(v):
    return v / (1.0 + jnp.exp(-v))


def face_weights(c):
    p = jnp.maximum(c, 0.0)
    w = jnp.maximum(-c, 0.0)
    alpha = 0.5 * p * p
    beta = 1.0 - 2.0 / 3.0 * p
    gamma = 0.5 * w * w
    delta = 1.0 - 2.0 / 3.0 * w
    x = alpha * (1.0 - 3.0 * beta)
    y = c - alpha * (1.0 + 3.0 * beta) + gamma * (1.0 + 3.0 * delta)
    z = -gamma * (1.0 - 3.0 * delta)
    u = 6.0 * alpha * beta
    v = -6.0 * gamma * delta
    a, b = 7.0 / 12.0, 1.0 / 12.0
    return [
        -b * x,
        a * x - b * y,
        a * (x + y) - b * z + u,
        a * (y + z) - b * x + v,
        a * z - b * y,
        -b * z,
    ]


def cell_weights(c, before):
    f, g = face_weights(c), face_weights(before)
    out = [g[0]]
    for m in range(5):
        out.append(g[m + 1] - f[m])
    out.append(-f[5])
    out[3] = out[3] + 1.0
    return out


def kernel(
    n_lat,
    n_lon,
    cap,
    *refs,
):
    given, refs = refs[:12], refs[12:]
    out_ref, held, refs = refs[0], refs[1:13], refs[13:]
    transport_step(n_lat, n_lon, cap, given, held, out_ref, *refs)


def transport_step(
    n_lat,
    n_lon,
    cap,
    given,
    held,
    out_ref,
    given_sem,
    zb,
    once_z,
    twice_z,
    wz,
    wk,
    mer_in,
    route_out,
    route_in,
    gm,
    st,
    fin,
    acc,
    slots,
    lon_sem,
    mer_sem,
    route_send,
    route_recv,
    lat_send,
    lat_recv,
):
    (
        feat_ref,
        tile_ref,
        spot_ref,
        w_in_ref,
        b_in_ref,
        w_mid_ref,
        b_mid_ref,
        w_out_ref,
        x_ref,
        zon_ref,
        mer_ref,
        mix_ref,
    ) = held
    lev, rows, _ = zon_ref.shape
    cells = feat_ref.shape[1]
    tr = st.shape[2]
    count = n_lat * n_lon
    groups = LANES // cap
    blocks = count // groups
    lat, lon = lax.axis_index("lat"), lax.axis_index("lon")
    me = lat * n_lon + lon
    west, east = lax.rem(lon + n_lon - 1, n_lon), lax.rem(lon + 1, n_lon)
    has_south, has_north = lat > 0, lat < n_lat - 1

    def place(d):
        return lax.rem(d, groups) * blocks + d // groups

    def load(i):
        return pltpu.make_async_copy(given[i], held[i], given_sem.at[i])

    for i in (8, 9, 10, 0, 3, 5, 4, 6, 7, 1, 2, 11):
        load(i).start()

    barrier = pltpu.get_barrier_semaphore()

    @pl.loop(1, count)
    def _(o):
        d = lax.rem(me + o, count)
        pl.semaphore_signal(
            barrier, inc=1, device_id=(d // n_lon, lax.rem(d, n_lon)), device_id_type=MESH
        )

    @pl.when(jnp.logical_not(has_south))
    def _():
        mer_in[1] = jnp.zeros((lev, rows, LANES), jnp.float32)

        @pl.loop(0, lev)
        def _(k):
            st[k, 0:WIDE] = jnp.zeros((WIDE, tr, LANES), jnp.float32)

    @pl.when(jnp.logical_not(has_north))
    def _():
        mer_in[0] = jnp.zeros((lev, rows, LANES), jnp.float32)

        @pl.loop(0, lev)
        def _(k):
            st[k, WIDE + rows :] = jnp.zeros((WIDE, tr, LANES), jnp.float32)

    load(8).wait()

    def halves(v):
        high = v.astype(jnp.bfloat16)
        low = (v - high.astype(jnp.float32)).astype(jnp.bfloat16)
        return jnp.concatenate([high, low], axis=1)

    def turned_by(order, v):
        return lax.dot_general(
            order, halves(v), (((1,), (1,)), ((), ())), preferred_element_type=jnp.float32
        )

    cell = lax.broadcasted_iota(jnp.int32, (LANES, 2 * LANES), 0)
    from_cell = lax.broadcasted_iota(jnp.int32, (LANES, 2 * LANES), 1) % LANES
    straight = (cell == from_cell).astype(jnp.float32).astype(jnp.bfloat16)
    by_row = (cell % tr * rows + cell // tr == from_cell).astype(jnp.float32).astype(jnp.bfloat16)
    own = slice(16, 16 + LANES)

    lead = lev - 3

    def turn_levels(start, stop):
        @pl.loop(start, stop)
        def _(k):
            zb[k, own] = turned_by(straight, x_ref[:, k].reshape(tr * rows, LANES))

    turn_levels(lead, lev)
    load(9).wait()
    zb[lev, own] = turned_by(straight, zon_ref[...].reshape(lev * rows, LANES))

    pl.semaphore_wait(barrier, count - 1)

    def lon_copy(part, side):
        levels = (pl.ds(lead, lev + 1 - lead), pl.ds(1, lead - 1), pl.ds(0, 1))[part]
        return pltpu.make_async_remote_copy(
            src_ref=zb.at[levels, pl.ds((16, 8 + LANES)[side], 8)],
            dst_ref=zb.at[levels, pl.ds((16 + LANES, 8)[side], 8)],
            send_sem=lon_sem.at[0, part, side],
            recv_sem=lon_sem.at[1, part, side],
            device_id=(lat, (west, east)[side]),
            device_id_type=MESH,
        )

    def mer_copy(side):
        return pltpu.make_async_remote_copy(
            src_ref=mer_ref,
            dst_ref=mer_in.at[side],
            send_sem=mer_sem.at[0, side],
            recv_sem=mer_sem.at[1, side],
            device_id=(lat + (-1, 1)[side], lon),
            device_id_type=MESH,
        )

    def lat_copy(k, side):
        return pltpu.make_async_remote_copy(
            src_ref=st.at[k, pl.ds((WIDE, rows)[side], WIDE)],
            dst_ref=st.at[k, pl.ds((WIDE + rows, 0)[side], WIDE)],
            send_sem=lat_send.at[side, k],
            recv_sem=lat_recv.at[side, k],
            device_id=(lat + (-1, 1)[side], lon),
            device_id_type=MESH,
        )

    def route_copy(d, origin):
        return pltpu.make_async_remote_copy(
            src_ref=route_out.at[place(d)],
            dst_ref=route_in.at[place(origin)],
            send_sem=route_send.at[d],
            recv_sem=route_recv.at[origin],
            device_id=(d // n_lon, lax.rem(d, n_lon)),
            device_id_type=MESH,
        )

    lon_copy(0, 0).start()
    lon_copy(0, 1).start()
    load(10).wait()

    @pl.when(has_south)
    def _():
        mer_copy(0).start()

    @pl.when(has_north)
    def _():
        mer_copy(1).start()

    turn_levels(1, lead)
    lon_copy(1, 0).start()
    lon_copy(1, 1).start()

    lon_copy(0, 0).wait_recv()
    lon_copy(0, 1).wait_recv()

    wide_cols = LANES + 16
    c = zb[lev, 8 : 8 + wide_cols]
    before = zb[lev, 7 : 7 + wide_cols]
    for m, weight in enumerate(cell_weights(c, before)):
        wz[m * wide_cols : (m + 1) * wide_cols] = halves(weight)
    pick_from = lax.broadcasted_iota(jnp.int32, (2 * LANES, LANES), 0) % LANES
    pick_row = lax.broadcasted_iota(jnp.int32, (2 * LANES, LANES), 1) % rows

    def zonal(k):
        pick = (pick_from == pick_row + k * rows).astype(jnp.float32).astype(jnp.bfloat16)
        for m in range(7):
            wk[m * wide_cols : (m + 1) * wide_cols] = jnp.dot(
                wz[m * wide_cols : (m + 1) * wide_cols], pick, preferred_element_type=jnp.float32
            )
        third = wide_cols // 3

        @pl.loop(0, 3)
        def _(i):
            new = 0.0
            for m in range(7):
                new = new + (
                    zb[k, pl.ds(i * third + 5 + m, third)]
                    * wk[pl.ds(pl.multiple_of(i * third + m * wide_cols, 8), third)]
                )
            once_z[pl.ds(pl.multiple_of(i * third + 8, 8), third)] = new

        half = LANES // 2

        @pl.loop(0, 2)
        def _(i):
            new = 0.0
            for m in range(7):
                new = new + (
                    once_z[pl.ds(i * half + 13 + m, half)]
                    * wk[pl.ds(pl.multiple_of(i * half + 8 + m * wide_cols, 8), half)]
                )
            twice_z[pl.ds(pl.multiple_of(i * half, 8), half)] = new

        st[k, WIDE : WIDE + rows] = turned_by(by_row, twice_z[...]).reshape(rows, tr, LANES)

    def send_rows(k):
        @pl.when(has_south)
        def _():
            lat_copy(k, 0).start()

        @pl.when(has_north)
        def _():
            lat_copy(k, 1).start()

    def blow(start, stop):
        @pl.loop(start, stop)
        def _(k):
            zonal(k)
            send_rows(k)

    blow(lead, lev)

    for i in (0, 3, 5, 4, 6, 7, 1, 2):
        load(i).wait()
    first = silu(
        lax.dot_general(
            feat_ref[...], w_in_ref[...], (((0,), (0,)), ((), ())), preferred_element_type=jnp.float32
        )
        + b_in_ref[...]
    ).astype(jnp.bfloat16)
    second = silu(
        jnp.dot(first, w_mid_ref[...], preferred_element_type=jnp.float32) + b_mid_ref[...]
    ).astype(jnp.bfloat16)
    flux = lax.dot_general(
        w_out_ref[...], second, (((1,), (1,)), ((), ())), preferred_element_type=jnp.float32
    )

    lon_copy(1, 0).wait_recv()
    lon_copy(1, 1).wait_recv()
    blow(1, lead // 2)

    tile = tile_ref[...]
    named = (tile == lax.broadcasted_iota(jnp.int32, (count, cells), 0)).astype(jnp.float32)
    ahead = (
        lax.broadcasted_iota(jnp.int32, (cells, cells), 0)
        < lax.broadcasted_iota(jnp.int32, (cells, cells), 1)
    ).astype(jnp.float32)
    rank = jnp.dot(
        named.astype(jnp.bfloat16), ahead.astype(jnp.bfloat16), preferred_element_type=jnp.float32
    )
    slot = jnp.sum(rank * named, axis=0, keepdims=True).astype(jnp.int32)
    key = tile * cap + slot
    spot = spot_ref[...]
    spots = jnp.where(
        lax.broadcasted_iota(jnp.int32, (16, cells), 0) == 0, spot // LANES, spot % LANES
    ).astype(jnp.float32)
    high = flux.astype(jnp.bfloat16)
    low = (flux - high.astype(jnp.float32)).astype(jnp.bfloat16)
    parts = jnp.concatenate([high, low, spots.astype(jnp.bfloat16)], axis=0)
    lane_of = lax.broadcasted_iota(jnp.int32, (LANES, cells), 0)

    @pl.loop(0, blocks)
    def _(j):
        taken = (key - j * LANES == lane_of).astype(jnp.float32).astype(jnp.bfloat16)
        placed = lax.dot_general(
            parts, taken, (((1,), (1,)), ((), ())), preferred_element_type=jnp.float32
        )
        summed = placed[0:tr] + placed[tr : 2 * tr]
        slots[0, j] = summed[0:8]
        slots[1, j] = summed[8:16]
        slots[2, j] = placed[2 * tr : 2 * tr + 8]

    stacked = [slots[h].reshape(8 * blocks, LANES) for h in range(3)]
    laneb = lax.broadcasted_iota(jnp.int32, (8 * blocks, LANES), 1)
    for g in range(groups):
        turned = [
            pltpu.roll(s, (cap * (h - g)) % LANES, 1) if h != g else s
            for h, s in enumerate(stacked)
        ]
        packed = jnp.where(laneb < cap, turned[0], jnp.where(laneb < 2 * cap, turned[1], turned[2]))
        route_out[blocks * g : blocks * (g + 1)] = packed.reshape(blocks, 8, LANES)

    @pl.loop(1, count)
    def _(o):
        route_copy(lax.rem(me + o, count), me).start()

    route_in[place(me)] = route_out[place(me)]

    blow(lead // 2, lead)

    @pl.when(has_south)
    def _():
        mer_copy(1).wait_recv()

    @pl.when(has_north)
    def _():
        mer_copy(0).wait_recv()

    grid_row = lax.broadcasted_iota(jnp.int32, (3 * rows, LANES), 0) + (lat - 1) * rows
    northern = (grid_row < n_lat * rows - 1).astype(jnp.float32)

    @pl.loop(0, lev)
    def _(k):
        c = jnp.concatenate([mer_in[1, k], mer_ref[k], mer_in[0, k]], axis=0) * northern
        for m, weight in enumerate(cell_weights(c, pltpu.roll(c, 1, 0))):
            gm[k, m] = weight

    @pl.loop(1, count)
    def _(o):
        route_copy(me, lax.rem(me + o, count)).wait_recv()

    lists = [jnp.zeros((8 * blocks, LANES), jnp.float32)] * 3
    for g in range(groups):
        got = route_in[blocks * g : blocks * (g + 1)].reshape(8 * blocks, LANES)
        for h in range(3):
            turned = pltpu.roll(got, (cap * (g - h)) % LANES, 1) if g != h else got
            lists[h] = jnp.where(laneb // cap == g, turned, lists[h])
    entries = [
        jnp.concatenate([part[8 * j : 8 * (j + 1)] for j in range(blocks)], axis=1)
        for part in lists
    ]
    values = jnp.concatenate(entries[:2], axis=0)
    at_row, at_lane = entries[2][0:1], entries[2][1:2]
    wide = blocks * LANES
    onto = (
        lax.broadcasted_iota(jnp.int32, (LANES, wide), 0).astype(jnp.float32) == at_lane
    ).astype(jnp.float32)
    row_of = lax.broadcasted_iota(jnp.int32, (rows, wide), 0).astype(jnp.float32)
    spread = jnp.concatenate(
        [jnp.where(at_row == row_of, values[t : t + 1], 0.0) for t in range(tr)], axis=0
    )
    high = spread.astype(jnp.bfloat16)
    low = (spread - high.astype(jnp.float32)).astype(jnp.bfloat16)
    emitted = lax.dot_general(
        jnp.concatenate([high, low], axis=0),
        onto.astype(jnp.bfloat16),
        (((1,), (1,)), ((), ())),
        preferred_element_type=jnp.float32,
    )
    emitted = emitted[: rows * tr] + emitted[rows * tr :]

    surface = x_ref[:, 0].reshape(tr * rows, LANES) + emitted
    zb[0, own] = turned_by(straight, surface)
    lon_copy(2, 0).start()
    lon_copy(2, 1).start()

    def meridional(k):
        @pl.when(has_south)
        def _():
            lat_copy(k, 1).wait_recv()

        @pl.when(has_north)
        def _():
            lat_copy(k, 0).wait_recv()

        once = []
        for a in range(-3, rows + 3):
            new = 0.0
            for m in range(7):
                new = new + st[k, a + 3 + m] * gm[k, m, a + rows : a + rows + 1]
            once.append(new)
        for a in range(rows):
            new = 0.0
            for m in range(7):
                new = new + once[a + m] * gm[k, m, a + rows : a + rows + 1]
            fin[k, a] = new

    def mixed(levels, opening, closing):
        @pl.loop(0, rows)
        def _(a):
            part = [fin[j, a] for j in levels]
            for k in range(lev):
                total = 0.0 if opening else acc[a, k]
                for j, value in zip(levels, part):
                    total = total + value * mix_ref[a, k, j]
                if closing:
                    out_ref[k, a] = total
                else:
                    acc[a, k] = total

    ordered = list(range(lead, lev)) + list(range(1, lead))
    share = len(ordered) // 3
    meet = lev - lead

    def some(i):
        levels = ordered[i * share : (i + 1) * share if i < 2 else None]
        first = 0

        if i == 0:

            @pl.loop(lead, lev)
            def _(k):
                meridional(k)

            first = meet

        @pl.loop(levels[first], levels[-1] + 1)
        def _(k):
            meridional(k)

        mixed(levels, i == 0, False)

    load(11).wait()
    some(0)
    lon_copy(2, 0).wait_recv()
    lon_copy(2, 1).wait_recv()
    zonal(0)
    send_rows(0)
    some(1)
    some(2)
    meridional(0)
    mixed(range(1), False, True)

    for side in range(2):
        for part in range(3):
            lon_copy(part, side).wait_send()

    @pl.loop(1, count)
    def _(o):
        route_copy(lax.rem(me + o, count), me).wait_send()

    @pl.when(has_south)
    def _():
        mer_copy(0).wait_send()

        @pl.loop(0, lev)
        def _(k):
            lat_copy(k, 0).wait_send()

    @pl.when(has_north)
    def _():
        mer_copy(1).wait_send()

        @pl.loop(0, lev)
        def _(k):
            lat_copy(k, 1).wait_send()


def on_device(
    n_lat,
    n_lon,
    features,
    land_tile,
    land_spot,
    w_in,
    b_in,
    w_mid,
    b_mid,
    w_out,
    tracers,
    zonal_wind,
    meridional_wind,
    mixing,
):
    tr, lev, rows, cols = tracers.shape
    cells = features.shape[0]
    count = n_lat * n_lon
    cap = 2 * cells // count
    f32 = jnp.float32
    args = (
        features.T,
        land_tile.T,
        land_spot.reshape(1, -1),
        w_in,
        b_in.reshape(1, -1),
        w_mid,
        b_mid.reshape(1, -1),
        w_out.T,
        tracers,
        zonal_wind,
        meridional_wind,
        mixing,
    )
    out = pl.pallas_call(
        functools.partial(kernel, n_lat, n_lon, cap),
        out_shape=jax.ShapeDtypeStruct((lev, rows, tr, cols), f32),
        in_specs=[pl.BlockSpec(memory_space=pltpu.HBM)] * len(args),
        out_specs=pl.BlockSpec(memory_space=pltpu.VMEM),
        scratch_shapes=[pltpu.VMEM(arg.shape, arg.dtype) for arg in args[:-1]]
        + [
            pltpu.SMEM(mixing.shape, f32),
            pltpu.SemaphoreType.DMA((len(args),)),
            pltpu.VMEM((lev + 1, cols + 32, tr * rows), f32),
            pltpu.VMEM((cols + 32, tr * rows), f32),
            pltpu.VMEM((cols, tr * rows), f32),
            pltpu.VMEM((7 * (cols + 16), 2 * lev * rows), jnp.bfloat16),
            pltpu.VMEM((7 * (cols + 16), tr * rows), f32),
            pltpu.VMEM((2, lev, rows, cols), f32),
            pltpu.VMEM((count, 8, cols), f32),
            pltpu.VMEM((count, 8, cols), f32),
            pltpu.VMEM((lev, 7, 3 * rows, cols), f32),
            pltpu.VMEM((lev, rows + 2 * WIDE, tr, cols), f32),
            pltpu.VMEM((lev, rows, tr, cols), f32),
            pltpu.VMEM((rows, lev, tr, cols), f32),
            pltpu.VMEM((3, count * cap // cols, 8, cols), f32),
            pltpu.SemaphoreType.DMA((2, 3, 2)),
            pltpu.SemaphoreType.DMA((2, 2)),
            pltpu.SemaphoreType.DMA((count,)),
            pltpu.SemaphoreType.DMA((count,)),
            pltpu.SemaphoreType.DMA((2, lev)),
            pltpu.SemaphoreType.DMA((2, lev)),
        ],
        compiler_params=pltpu.CompilerParams(
            collective_id=0, has_side_effects=True, vmem_limit_bytes=60 * 1024 * 1024
        ),
    )(*args)
    return out.transpose(2, 0, 1, 3)


def solution(mesh):
    placed = (
        P(("lat", "lon"), None),
        P(("lat", "lon"), None),
        P(("lat", "lon")),
        P(),
        P(),
        P(),
        P(),
        P(),
        P(None, None, "lat", "lon"),
        P(None, "lat", "lon"),
        P(None, "lat", "lon"),
        P("lat", None, None),
    )
    return jax.shard_map(
        functools.partial(on_device, mesh.shape["lat"], mesh.shape["lon"]),
        mesh=mesh,
        in_specs=placed,
        out_specs=P(None, None, "lat", "lon"),
        check_vma=False,
    )
```

```python
import functools

import jax
import jax.numpy as jnp
from jax import lax
from jax.experimental import pallas as pl
from jax.experimental.pallas import tpu as pltpu
from jax.sharding import PartitionSpec as P

MESH = pl.DeviceIdType.MESH
LANES = 128
WIDE = 6


def silu(v):
    half = 0.5 * v
    return half + half * jnp.tanh(half)


def face_weights(c):
    p = jnp.maximum(c, 0.0)
    w = jnp.maximum(-c, 0.0)
    alpha = 0.5 * p * p
    beta = 1.0 - 2.0 / 3.0 * p
    gamma = 0.5 * w * w
    delta = 1.0 - 2.0 / 3.0 * w
    x = alpha * (1.0 - 3.0 * beta)
    y = c - alpha * (1.0 + 3.0 * beta) + gamma * (1.0 + 3.0 * delta)
    z = -gamma * (1.0 - 3.0 * delta)
    u = 6.0 * alpha * beta
    v = -6.0 * gamma * delta
    a, b = 7.0 / 12.0, 1.0 / 12.0
    return [
        -b * x,
        a * x - b * y,
        a * (x + y) - b * z + u,
        a * (y + z) - b * x + v,
        a * z - b * y,
        -b * z,
    ]


def cell_weights(c, before):
    f, g = face_weights(c), face_weights(before)
    out = [g[0]]
    for m in range(5):
        out.append(g[m + 1] - f[m])
    out.append(-f[5])
    out[3] = out[3] + 1.0
    return out


def kernel(
    n_lat,
    n_lon,
    cap,
    *refs,
):
    given, refs = refs[:12], refs[12:]
    out_ref, held, refs = refs[0], refs[1:13], refs[13:]
    transport_step(n_lat, n_lon, cap, given, held, out_ref, *refs)


def transport_step(
    n_lat,
    n_lon,
    cap,
    given,
    held,
    out_ref,
    given_sem,
    zb,
    once_z,
    twice_z,
    wz,
    wk,
    mer_in,
    route_out,
    route_in,
    gm,
    st,
    fin,
    acc,
    slots,
    lon_sem,
    mer_sem,
    route_send,
    route_recv,
    lat_send,
    lat_recv,
    out_sem,
):
    (
        feat_ref,
        tile_ref,
        spot_ref,
        w_in_ref,
        b_in_ref,
        w_mid_ref,
        b_mid_ref,
        w_out_ref,
        x_ref,
        zon_ref,
        mer_ref,
        mix_ref,
    ) = held
    lev, rows, _ = zon_ref.shape
    cells = feat_ref.shape[1]
    tr = st.shape[2]
    count = n_lat * n_lon
    groups = LANES // cap
    blocks = count // groups
    lat, lon = lax.axis_index("lat"), lax.axis_index("lon")
    me = lat * n_lon + lon
    west, east = lax.rem(lon + n_lon - 1, n_lon), lax.rem(lon + 1, n_lon)
    has_south, has_north = lat > 0, lat < n_lat - 1

    def place(d):
        return lax.rem(d, groups) * blocks + d // groups

    def load(i):
        return pltpu.make_async_copy(given[i], held[i], given_sem.at[i])

    for i in (8, 9, 10, 0, 3, 5, 4, 6, 7, 1, 2, 11):
        load(i).start()

    barrier = pltpu.get_barrier_semaphore()

    @pl.loop(1, count)
    def _(o):
        d = lax.rem(me + o, count)
        pl.semaphore_signal(
            barrier, inc=1, device_id=(d // n_lon, lax.rem(d, n_lon)), device_id_type=MESH
        )

    @pl.when(jnp.logical_not(has_south))
    def _():
        mer_in[1] = jnp.zeros((lev, rows, LANES), jnp.float32)

        @pl.loop(0, lev)
        def _(k):
            st[k, 0:WIDE] = jnp.zeros((WIDE, tr, LANES), jnp.float32)

    @pl.when(jnp.logical_not(has_north))
    def _():
        mer_in[0] = jnp.zeros((lev, rows, LANES), jnp.float32)

        @pl.loop(0, lev)
        def _(k):
            st[k, WIDE + rows :] = jnp.zeros((WIDE, tr, LANES), jnp.float32)

    load(8).wait()

    def halves(v):
        high = v.astype(jnp.bfloat16)
        low = (v - high.astype(jnp.float32)).astype(jnp.bfloat16)
        return jnp.concatenate([high, low], axis=1)

    def turned_by(order, v):
        return lax.dot_general(
            order, halves(v), (((1,), (1,)), ((), ())), preferred_element_type=jnp.float32
        )

    cell = lax.broadcasted_iota(jnp.int32, (LANES, 2 * LANES), 0)
    from_cell = lax.broadcasted_iota(jnp.int32, (LANES, 2 * LANES), 1) % LANES
    straight = (cell == from_cell).astype(jnp.float32).astype(jnp.bfloat16)
    by_row = (cell % tr * rows + cell // tr == from_cell).astype(jnp.float32).astype(jnp.bfloat16)
    own = slice(16, 16 + LANES)

    lead = lev - 3

    def turn_levels(start, stop):
        @pl.loop(start, stop)
        def _(k):
            zb[k, own] = turned_by(straight, x_ref[:, k].reshape(tr * rows, LANES))

    turn_levels(lead, lev)
    load(9).wait()
    zb[lev, own] = turned_by(straight, zon_ref[...].reshape(lev * rows, LANES))

    pl.semaphore_wait(barrier, count - 1)

    def lon_copy(part, side):
        levels = (pl.ds(lead, lev + 1 - lead), pl.ds(1, lead - 1), pl.ds(0, 1))[part]
        return pltpu.make_async_remote_copy(
            src_ref=zb.at[levels, pl.ds((16, 8 + LANES)[side], 8)],
            dst_ref=zb.at[levels, pl.ds((16 + LANES, 8)[side], 8)],
            send_sem=lon_sem.at[0, part, side],
            recv_sem=lon_sem.at[1, part, side],
            device_id=(lat, (west, east)[side]),
            device_id_type=MESH,
        )

    def mer_copy(side):
        return pltpu.make_async_remote_copy(
            src_ref=mer_ref,
            dst_ref=mer_in.at[side],
            send_sem=mer_sem.at[0, side],
            recv_sem=mer_sem.at[1, side],
            device_id=(lat + (-1, 1)[side], lon),
            device_id_type=MESH,
        )

    def lat_copy(k, side):
        return pltpu.make_async_remote_copy(
            src_ref=st.at[k, pl.ds((WIDE, rows)[side], WIDE)],
            dst_ref=st.at[k, pl.ds((WIDE + rows, 0)[side], WIDE)],
            send_sem=lat_send.at[side],
            recv_sem=lat_recv.at[side, k],
            device_id=(lat + (-1, 1)[side], lon),
            device_id_type=MESH,
        )

    def lat_all(side):
        return pltpu.make_async_remote_copy(
            src_ref=st.at[:, pl.ds((WIDE, rows)[side], WIDE)],
            dst_ref=st.at[:, pl.ds((WIDE + rows, 0)[side], WIDE)],
            send_sem=lat_send.at[side],
            recv_sem=lat_recv.at[side, 0],
            device_id=(lat + (-1, 1)[side], lon),
            device_id_type=MESH,
        )

    def route_all():
        return pltpu.make_async_remote_copy(
            src_ref=route_out.at[pl.ds(0, count - 1)],
            dst_ref=route_in.at[pl.ds(0, count - 1)],
            send_sem=route_send.at[0],
            recv_sem=route_recv.at[0],
            device_id=(lat, east),
            device_id_type=MESH,
        )

    def route_copy(d, origin):
        return pltpu.make_async_remote_copy(
            src_ref=route_out.at[place(d)],
            dst_ref=route_in.at[place(origin)],
            send_sem=route_send.at[0],
            recv_sem=route_recv.at[0],
            device_id=(d // n_lon, lax.rem(d, n_lon)),
            device_id_type=MESH,
        )

    lon_copy(0, 0).start()
    lon_copy(0, 1).start()
    load(10).wait()

    @pl.when(has_south)
    def _():
        mer_copy(0).start()

    @pl.when(has_north)
    def _():
        mer_copy(1).start()

    turn_levels(1, lead)
    lon_copy(1, 0).start()
    lon_copy(1, 1).start()

    lon_copy(0, 0).wait_recv()
    lon_copy(0, 1).wait_recv()

    wide_cols = LANES + 16
    c = zb[lev, 8 : 8 + wide_cols]
    before = zb[lev, 7 : 7 + wide_cols]
    for m, weight in enumerate(cell_weights(c, before)):
        wz[m * wide_cols : (m + 1) * wide_cols] = halves(weight)
    pick_from = lax.broadcasted_iota(jnp.int32, (2 * LANES, LANES), 0) % LANES
    pick_row = lax.broadcasted_iota(jnp.int32, (2 * LANES, LANES), 1) % rows

    def zonal(k):
        pick = (pick_from == pick_row + k * rows).astype(jnp.float32).astype(jnp.bfloat16)
        for m in range(7):
            wk[m * wide_cols : (m + 1) * wide_cols] = jnp.dot(
                wz[m * wide_cols : (m + 1) * wide_cols], pick, preferred_element_type=jnp.float32
            )
        third = wide_cols // 3

        @pl.loop(0, 3)
        def _(i):
            new = 0.0
            for m in range(7):
                new = new + (
                    zb[k, pl.ds(i * third + 5 + m, third)]
                    * wk[pl.ds(pl.multiple_of(i * third + m * wide_cols, 8), third)]
                )
            once_z[pl.ds(pl.multiple_of(i * third + 8, 8), third)] = new

        half = LANES // 2

        @pl.loop(0, 2)
        def _(i):
            new = 0.0
            for m in range(7):
                new = new + (
                    once_z[pl.ds(i * half + 13 + m, half)]
                    * wk[pl.ds(pl.multiple_of(i * half + 8 + m * wide_cols, 8), half)]
                )
            twice_z[pl.ds(pl.multiple_of(i * half, 8), half)] = new

        st[k, WIDE : WIDE + rows] = turned_by(by_row, twice_z[...]).reshape(rows, tr, LANES)

    def send_rows(k):
        @pl.when(has_south)
        def _():
            lat_copy(k, 0).start()

        @pl.when(has_north)
        def _():
            lat_copy(k, 1).start()

    def blow(start, stop):
        @pl.loop(start, stop)
        def _(k):
            zonal(k)
            send_rows(k)

    blow(lead, lev)

    for i in (0, 3, 5, 4, 6, 7, 1, 2):
        load(i).wait()
    first = silu(
        lax.dot_general(
            feat_ref[...], w_in_ref[...], (((0,), (0,)), ((), ())), preferred_element_type=jnp.float32
        )
        + b_in_ref[...]
    ).astype(jnp.bfloat16)
    second = silu(
        jnp.dot(first, w_mid_ref[...], preferred_element_type=jnp.float32) + b_mid_ref[...]
    ).astype(jnp.bfloat16)
    flux = lax.dot_general(
        w_out_ref[...], second, (((1,), (1,)), ((), ())), preferred_element_type=jnp.float32
    )

    lon_copy(1, 0).wait_recv()
    lon_copy(1, 1).wait_recv()
    blow(1, lead // 2)

    tile = tile_ref[...]
    named = (tile == lax.broadcasted_iota(jnp.int32, (count, cells), 0)).astype(jnp.float32)
    ahead = (
        lax.broadcasted_iota(jnp.int32, (cells, cells), 0)
        < lax.broadcasted_iota(jnp.int32, (cells, cells), 1)
    ).astype(jnp.float32)
    rank = jnp.dot(
        named.astype(jnp.bfloat16), ahead.astype(jnp.bfloat16), preferred_element_type=jnp.float32
    )
    slot = jnp.sum(rank * named, axis=0, keepdims=True).astype(jnp.int32)
    key = tile * cap + slot
    spot = spot_ref[...]
    spots = jnp.where(
        lax.broadcasted_iota(jnp.int32, (16, cells), 0) == 0, spot // LANES, spot % LANES
    ).astype(jnp.float32)
    high = flux.astype(jnp.bfloat16)
    low = (flux - high.astype(jnp.float32)).astype(jnp.bfloat16)
    parts = jnp.concatenate([high, low, spots.astype(jnp.bfloat16)], axis=0)
    lane_of = lax.broadcasted_iota(jnp.int32, (LANES, cells), 0)

    @pl.loop(0, blocks)
    def _(j):
        taken = (key - j * LANES == lane_of).astype(jnp.float32).astype(jnp.bfloat16)
        placed = lax.dot_general(
            parts, taken, (((1,), (1,)), ((), ())), preferred_element_type=jnp.float32
        )
        summed = placed[0:tr] + placed[tr : 2 * tr]
        slots[0, j] = summed[0:8]
        slots[1, j] = summed[8:16]
        slots[2, j] = placed[2 * tr : 2 * tr + 8]

    stacked = [slots[h].reshape(8 * blocks, LANES) for h in range(3)]
    laneb = lax.broadcasted_iota(jnp.int32, (8 * blocks, LANES), 1)
    for g in range(groups):
        turned = [
            pltpu.roll(s, (cap * (h - g)) % LANES, 1) if h != g else s
            for h, s in enumerate(stacked)
        ]
        packed = jnp.where(laneb < cap, turned[0], jnp.where(laneb < 2 * cap, turned[1], turned[2]))
        route_out[blocks * g : blocks * (g + 1)] = packed.reshape(blocks, 8, LANES)

    @pl.loop(1, count)
    def _(o):
        route_copy(lax.rem(me + o, count), me).start()

    route_in[place(me)] = route_out[place(me)]

    blow(lead // 2, lead)

    @pl.when(has_south)
    def _():
        mer_copy(1).wait_recv()

    @pl.when(has_north)
    def _():
        mer_copy(0).wait_recv()

    grid_row = lax.broadcasted_iota(jnp.int32, (3 * rows, LANES), 0) + (lat - 1) * rows
    northern = (grid_row < n_lat * rows - 1).astype(jnp.float32)

    @pl.loop(0, lev)
    def _(k):
        c = jnp.concatenate([mer_in[1, k], mer_ref[k], mer_in[0, k]], axis=0) * northern
        for m, weight in enumerate(cell_weights(c, pltpu.roll(c, 1, 0))):
            gm[k, m, 0 : 3 * rows] = weight

    route_all().wait_recv()
    route_all().wait_send()

    lists = [jnp.zeros((8 * blocks, LANES), jnp.float32)] * 3
    for g in range(groups):
        got = route_in[blocks * g : blocks * (g + 1)].reshape(8 * blocks, LANES)
        for h in range(3):
            turned = pltpu.roll(got, (cap * (g - h)) % LANES, 1) if g != h else got
            lists[h] = jnp.where(laneb // cap == g, turned, lists[h])
    entries = [
        jnp.concatenate([part[8 * j : 8 * (j + 1)] for j in range(blocks)], axis=1)
        for part in lists
    ]
    values = jnp.concatenate(entries[:2], axis=0)
    at_row, at_lane = entries[2][0:1], entries[2][1:2]
    wide = blocks * LANES
    onto = (
        lax.broadcasted_iota(jnp.int32, (LANES, wide), 0).astype(jnp.float32) == at_lane
    ).astype(jnp.float32)
    row_of = lax.broadcasted_iota(jnp.int32, (rows, wide), 0).astype(jnp.float32)
    spread = jnp.concatenate(
        [jnp.where(at_row == row_of, values[t : t + 1], 0.0) for t in range(tr)], axis=0
    )
    high = spread.astype(jnp.bfloat16)
    low = (spread - high.astype(jnp.float32)).astype(jnp.bfloat16)
    emitted = lax.dot_general(
        jnp.concatenate([high, low], axis=0),
        onto.astype(jnp.bfloat16),
        (((1,), (1,)), ((), ())),
        preferred_element_type=jnp.float32,
    )
    emitted = emitted[: rows * tr] + emitted[rows * tr :]

    surface = x_ref[:, 0].reshape(tr * rows, LANES) + emitted
    zb[0, own] = turned_by(straight, surface)
    lon_copy(2, 0).start()
    lon_copy(2, 1).start()

    def meridional(k):
        @pl.when(has_south)
        def _():
            lat_copy(k, 1).wait_recv()

        @pl.when(has_north)
        def _():
            lat_copy(k, 0).wait_recv()

        once = []
        for a in range(-3, rows + 3):
            new = 0.0
            for m in range(7):
                new = new + st[k, a + 3 + m] * gm[k, m, pl.ds(a + rows, tr, stride=0), :]
            once.append(new)
        for a in range(rows):
            new = 0.0
            for m in range(7):
                new = new + once[a + m] * gm[k, m, pl.ds(a + rows, tr, stride=0), :]
            fin[k, a] = new

    def mixed(levels, opening, closing):
        @pl.loop(0, rows)
        def _(a):
            part = [fin[j, a] for j in levels]
            for k in range(lev):
                total = 0.0 if opening else acc[a, k]
                for j, value in zip(levels, part):
                    total = total + value * mix_ref[a, k, j]
                acc[a, k] = total
            if closing:
                pltpu.make_async_copy(acc.at[a], out_ref.at[a], out_sem.at[a]).start()

    ordered = list(range(lead, lev)) + list(range(1, lead))
    share = len(ordered) // 3
    meet = lev - lead

    def some(i):
        levels = ordered[i * share : (i + 1) * share if i < 2 else None]
        first = 0

        if i == 0:

            @pl.loop(lead, lev)
            def _(k):
                meridional(k)

            first = meet

        @pl.loop(levels[first], levels[-1] + 1)
        def _(k):
            meridional(k)

        mixed(levels, i == 0, False)

    load(11).wait()
    some(0)
    lon_copy(2, 0).wait_recv()
    lon_copy(2, 1).wait_recv()
    zonal(0)
    send_rows(0)
    some(1)
    some(2)
    meridional(0)
    mixed(range(1), False, True)

    @pl.loop(0, rows)
    def _(a):
        pltpu.make_async_copy(acc.at[a], out_ref.at[a], out_sem.at[a]).wait()

    for side in range(2):
        for part in range(3):
            lon_copy(part, side).wait_send()

    @pl.when(has_south)
    def _():
        mer_copy(0).wait_send()
        lat_all(0).wait_send()

    @pl.when(has_north)
    def _():
        mer_copy(1).wait_send()
        lat_all(1).wait_send()


def on_device(
    n_lat,
    n_lon,
    features,
    land_tile,
    land_spot,
    w_in,
    b_in,
    w_mid,
    b_mid,
    w_out,
    tracers,
    zonal_wind,
    meridional_wind,
    mixing,
):
    tr, lev, rows, cols = tracers.shape
    cells = features.shape[0]
    count = n_lat * n_lon
    cap = 2 * cells // count
    f32 = jnp.float32
    args = (
        features.T,
        land_tile.T,
        land_spot.reshape(1, -1),
        w_in,
        b_in.reshape(1, -1),
        w_mid,
        b_mid.reshape(1, -1),
        w_out.T,
        tracers,
        zonal_wind,
        meridional_wind,
        mixing,
    )
    out = pl.pallas_call(
        functools.partial(kernel, n_lat, n_lon, cap),
        out_shape=jax.ShapeDtypeStruct((rows, lev, tr, cols), f32),
        in_specs=[pl.BlockSpec(memory_space=pltpu.HBM)] * len(args),
        out_specs=pl.BlockSpec(memory_space=pltpu.HBM),
        scratch_shapes=[pltpu.VMEM(arg.shape, arg.dtype) for arg in args[:-1]]
        + [
            pltpu.SMEM(mixing.shape, f32),
            pltpu.SemaphoreType.DMA((len(args),)),
            pltpu.VMEM((lev + 1, cols + 32, tr * rows), f32),
            pltpu.VMEM((cols + 32, tr * rows), f32),
            pltpu.VMEM((cols, tr * rows), f32),
            pltpu.VMEM((7 * (cols + 16), 2 * lev * rows), jnp.bfloat16),
            pltpu.VMEM((7 * (cols + 16), tr * rows), f32),
            pltpu.VMEM((2, lev, rows, cols), f32),
            pltpu.VMEM((count, 8, cols), f32),
            pltpu.VMEM((count, 8, cols), f32),
            pltpu.VMEM((lev, 7, 3 * rows + tr, cols), f32),
            pltpu.VMEM((lev, rows + 2 * WIDE, tr, cols), f32),
            pltpu.VMEM((lev, rows, tr, cols), f32),
            pltpu.VMEM((rows, lev, tr, cols), f32),
            pltpu.VMEM((3, count * cap // cols, 8, cols), f32),
            pltpu.SemaphoreType.DMA((2, 3, 2)),
            pltpu.SemaphoreType.DMA((2, 2)),
            pltpu.SemaphoreType.DMA((1,)),
            pltpu.SemaphoreType.DMA((1,)),
            pltpu.SemaphoreType.DMA((2,)),
            pltpu.SemaphoreType.DMA((2, lev)),
            pltpu.SemaphoreType.DMA((rows,)),
        ],
        compiler_params=pltpu.CompilerParams(
            collective_id=0, has_side_effects=True, vmem_limit_bytes=60 * 1024 * 1024
        ),
    )(*args)
    return out.transpose(2, 1, 0, 3)


def solution(mesh):
    placed = (
        P(("lat", "lon"), None),
        P(("lat", "lon"), None),
        P(("lat", "lon")),
        P(),
        P(),
        P(),
        P(),
        P(),
        P(None, None, "lat", "lon"),
        P(None, "lat", "lon"),
        P(None, "lat", "lon"),
        P("lat", None, None),
    )
    return jax.shard_map(
        functools.partial(on_device, mesh.shape["lat"], mesh.shape["lon"]),
        mesh=mesh,
        in_specs=placed,
        out_specs=P(None, None, "lat", "lon"),
        check_vma=False,
    )
```

```python
import functools

import jax
import jax.numpy as jnp
from jax import lax
from jax.experimental import pallas as pl
from jax.experimental.pallas import tpu as pltpu
from jax.sharding import PartitionSpec as P

MESH = pl.DeviceIdType.MESH
LANES = 128
WIDE = 6


def silu(v):
    half = 0.5 * v
    return half + half * jnp.tanh(half)


def face_weights(c):
    p = jnp.maximum(c, 0.0)
    w = jnp.maximum(-c, 0.0)
    alpha = 0.5 * p * p
    beta = 1.0 - 2.0 / 3.0 * p
    gamma = 0.5 * w * w
    delta = 1.0 - 2.0 / 3.0 * w
    x = alpha * (1.0 - 3.0 * beta)
    y = c - alpha * (1.0 + 3.0 * beta) + gamma * (1.0 + 3.0 * delta)
    z = -gamma * (1.0 - 3.0 * delta)
    u = 6.0 * alpha * beta
    v = -6.0 * gamma * delta
    a, b = 7.0 / 12.0, 1.0 / 12.0
    return [
        -b * x,
        a * x - b * y,
        a * (x + y) - b * z + u,
        a * (y + z) - b * x + v,
        a * z - b * y,
        -b * z,
    ]


def cell_weights(c, before):
    f, g = face_weights(c), face_weights(before)
    out = [g[0]]
    for m in range(5):
        out.append(g[m + 1] - f[m])
    out.append(-f[5])
    out[3] = out[3] + 1.0
    return out


def kernel(
    n_lat,
    n_lon,
    cap,
    *refs,
):
    given, refs = refs[:12], refs[12:]
    out_ref, held, refs = refs[0], refs[1:13], refs[13:]
    transport_step(n_lat, n_lon, cap, given, held, out_ref, *refs)


def transport_step(
    n_lat,
    n_lon,
    cap,
    given,
    held,
    out_ref,
    given_sem,
    zb,
    once_z,
    twice_z,
    wz,
    wk,
    mer_in,
    route_out,
    route_in,
    gm,
    st,
    fin,
    acc,
    slots,
    lon_sem,
    mer_sem,
    route_send,
    route_recv,
    lat_send,
    lat_recv,
    out_sem,
):
    (
        feat_ref,
        tile_ref,
        spot_ref,
        w_in_ref,
        b_in_ref,
        w_mid_ref,
        b_mid_ref,
        w_out_ref,
        x_ref,
        zon_ref,
        mer_ref,
        mix_ref,
    ) = held
    lev, rows, _ = zon_ref.shape
    cells = feat_ref.shape[1]
    tr = st.shape[2]
    count = n_lat * n_lon
    groups = LANES // cap
    blocks = count // groups
    lat, lon = lax.axis_index("lat"), lax.axis_index("lon")
    me = lat * n_lon + lon
    west, east = lax.rem(lon + n_lon - 1, n_lon), lax.rem(lon + 1, n_lon)
    has_south, has_north = lat > 0, lat < n_lat - 1

    def place(d):
        return lax.rem(d, groups) * blocks + d // groups

    def load(i):
        return pltpu.make_async_copy(given[i], held[i], given_sem.at[i])

    for i in (8, 9, 10, 0, 3, 5, 4, 6, 7, 1, 2, 11):
        load(i).start()

    barrier = pltpu.get_barrier_semaphore()

    @pl.loop(1, count)
    def _(o):
        d = lax.rem(me + o, count)
        pl.semaphore_signal(
            barrier, inc=1, device_id=(d // n_lon, lax.rem(d, n_lon)), device_id_type=MESH
        )

    @pl.when(jnp.logical_not(has_south))
    def _():
        mer_in[1] = jnp.zeros((lev, rows, LANES), jnp.float32)

        @pl.loop(0, lev)
        def _(k):
            st[k, 0:WIDE] = jnp.zeros((WIDE, tr, LANES), jnp.float32)

    @pl.when(jnp.logical_not(has_north))
    def _():
        mer_in[0] = jnp.zeros((lev, rows, LANES), jnp.float32)

        @pl.loop(0, lev)
        def _(k):
            st[k, WIDE + rows :] = jnp.zeros((WIDE, tr, LANES), jnp.float32)

    load(8).wait()

    def halves(v):
        high = v.astype(jnp.bfloat16)
        low = (v - high.astype(jnp.float32)).astype(jnp.bfloat16)
        return jnp.concatenate([high, low], axis=1)

    def turned_by(order, v):
        return lax.dot_general(
            order, halves(v), (((1,), (1,)), ((), ())), preferred_element_type=jnp.float32
        )

    cell = lax.broadcasted_iota(jnp.int32, (LANES, 2 * LANES), 0)
    from_cell = lax.broadcasted_iota(jnp.int32, (LANES, 2 * LANES), 1) % LANES
    straight = (cell == from_cell).astype(jnp.float32).astype(jnp.bfloat16)
    by_row = (cell % tr * rows + cell // tr == from_cell).astype(jnp.float32).astype(jnp.bfloat16)
    own = slice(16, 16 + LANES)

    lead = lev - 4

    def turn_levels(start, stop):
        @pl.loop(start, stop, unroll=4 if (stop - start) % 4 == 0 else stop - start)
        def _(k):
            zb[k, own] = turned_by(straight, x_ref[:, k].reshape(tr * rows, LANES))

    turn_levels(lead, lev)
    load(9).wait()
    zb[lev, own] = turned_by(straight, zon_ref[...].reshape(lev * rows, LANES))

    pl.semaphore_wait(barrier, count - 1)

    def lon_copy(part, side):
        levels = (pl.ds(lead, lev + 1 - lead), pl.ds(1, lead - 1), pl.ds(0, 1))[part]
        return pltpu.make_async_remote_copy(
            src_ref=zb.at[levels, pl.ds((16, 8 + LANES)[side], 8)],
            dst_ref=zb.at[levels, pl.ds((16 + LANES, 8)[side], 8)],
            send_sem=lon_sem.at[0, part, side],
            recv_sem=lon_sem.at[1, part, side],
            device_id=(lat, (west, east)[side]),
            device_id_type=MESH,
        )

    def mer_copy(side):
        return pltpu.make_async_remote_copy(
            src_ref=mer_ref,
            dst_ref=mer_in.at[side],
            send_sem=mer_sem.at[0, side],
            recv_sem=mer_sem.at[1, side],
            device_id=(lat + (-1, 1)[side], lon),
            device_id_type=MESH,
        )

    def lat_copy(k, side):
        return pltpu.make_async_remote_copy(
            src_ref=st.at[k, pl.ds((WIDE, rows)[side], WIDE)],
            dst_ref=st.at[k, pl.ds((WIDE + rows, 0)[side], WIDE)],
            send_sem=lat_send.at[side],
            recv_sem=lat_recv.at[side, k],
            device_id=(lat + (-1, 1)[side], lon),
            device_id_type=MESH,
        )

    def lat_all(side):
        return pltpu.make_async_remote_copy(
            src_ref=st.at[:, pl.ds((WIDE, rows)[side], WIDE)],
            dst_ref=st.at[:, pl.ds((WIDE + rows, 0)[side], WIDE)],
            send_sem=lat_send.at[side],
            recv_sem=lat_recv.at[side, 0],
            device_id=(lat + (-1, 1)[side], lon),
            device_id_type=MESH,
        )

    def route_all():
        return pltpu.make_async_remote_copy(
            src_ref=route_out.at[pl.ds(0, count - 1)],
            dst_ref=route_in.at[pl.ds(0, count - 1)],
            send_sem=route_send.at[0],
            recv_sem=route_recv.at[0],
            device_id=(lat, east),
            device_id_type=MESH,
        )

    def route_copy(d, origin):
        return pltpu.make_async_remote_copy(
            src_ref=route_out.at[place(d)],
            dst_ref=route_in.at[place(origin)],
            send_sem=route_send.at[0],
            recv_sem=route_recv.at[0],
            device_id=(d // n_lon, lax.rem(d, n_lon)),
            device_id_type=MESH,
        )

    lon_copy(0, 0).start()
    lon_copy(0, 1).start()
    load(10).wait()

    @pl.when(has_south)
    def _():
        mer_copy(0).start()

    @pl.when(has_north)
    def _():
        mer_copy(1).start()

    turn_levels(1, lead)
    lon_copy(1, 0).start()
    lon_copy(1, 1).start()

    lon_copy(0, 0).wait_recv()
    lon_copy(0, 1).wait_recv()

    wide_cols = LANES + 16
    c = zb[lev, 8 : 8 + wide_cols]
    before = zb[lev, 7 : 7 + wide_cols]
    for m, weight in enumerate(cell_weights(c, before)):
        wz[m * wide_cols : (m + 1) * wide_cols] = halves(weight)
    third = wide_cols // 3
    half = LANES // 2

    def zonal(k, number):
        lanes = [slice(j * LANES, (j + 1) * LANES) for j in range(number)]
        shape = (2 * LANES, number * LANES)
        pick_from = lax.broadcasted_iota(jnp.int32, shape, 0) % LANES
        at = lax.broadcasted_iota(jnp.int32, shape, 1)
        pick = pick_from == at % rows + (k + at // LANES) * rows
        pick = pick.astype(jnp.float32).astype(jnp.bfloat16)
        for m in range(7):
            wk[m * wide_cols : (m + 1) * wide_cols, : number * LANES] = jnp.dot(
                wz[m * wide_cols : (m + 1) * wide_cols], pick, preferred_element_type=jnp.float32
            )

        @pl.loop(0, 3)
        def _(i):
            for j in range(number):
                new = 0.0
                for m in range(7):
                    new = new + (
                        zb[k + j, pl.ds(i * third + 5 + m, third)]
                        * wk[pl.ds(pl.multiple_of(i * third + m * wide_cols, 8), third), lanes[j]]
                    )
                once_z[j, pl.ds(pl.multiple_of(i * third + 8, 8), third)] = new

        @pl.loop(0, 2)
        def _(i):
            for j in range(number):
                new = 0.0
                for m in range(7):
                    new = new + (
                        once_z[j, pl.ds(i * half + 13 + m, half)]
                        * wk[pl.ds(pl.multiple_of(i * half + 8 + m * wide_cols, 8), half), lanes[j]]
                    )
                twice_z[j, pl.ds(pl.multiple_of(i * half, 8), half)] = new

        for j in range(number):
            st[k + j, WIDE : WIDE + rows] = turned_by(by_row, twice_z[j]).reshape(rows, tr, LANES)

    def send_rows(k):
        @pl.when(has_south)
        def _():
            lat_copy(k, 0).start()

        @pl.when(has_north)
        def _():
            lat_copy(k, 1).start()

    def blow(start, stop):
        @pl.loop(0, (stop - start) // 2)
        def _(i):
            k = start + 2 * i
            zonal(k, 2)
            send_rows(k)
            send_rows(k + 1)

        if (stop - start) % 2:
            zonal(stop - 1, 1)
            send_rows(stop - 1)

    blow(lead, lev)

    for i in (0, 3, 5, 4, 6, 7, 1, 2):
        load(i).wait()
    first = silu(
        lax.dot_general(
            feat_ref[...], w_in_ref[...], (((0,), (0,)), ((), ())), preferred_element_type=jnp.float32
        )
        + b_in_ref[...]
    ).astype(jnp.bfloat16)
    second = silu(
        jnp.dot(first, w_mid_ref[...], preferred_element_type=jnp.float32) + b_mid_ref[...]
    ).astype(jnp.bfloat16)
    flux = lax.dot_general(
        w_out_ref[...], second, (((1,), (1,)), ((), ())), preferred_element_type=jnp.float32
    )

    lon_copy(1, 0).wait_recv()
    lon_copy(1, 1).wait_recv()
    blow(1, lead // 2 + 1)

    tile = tile_ref[...]
    named = (tile == lax.broadcasted_iota(jnp.int32, (count, cells), 0)).astype(jnp.float32)
    ahead = (
        lax.broadcasted_iota(jnp.int32, (cells, cells), 0)
        < lax.broadcasted_iota(jnp.int32, (cells, cells), 1)
    ).astype(jnp.float32)
    rank = jnp.dot(
        named.astype(jnp.bfloat16), ahead.astype(jnp.bfloat16), preferred_element_type=jnp.float32
    )
    slot = jnp.sum(rank * named, axis=0, keepdims=True).astype(jnp.int32)
    key = tile * cap + slot
    spot = spot_ref[...]
    spots = jnp.where(
        lax.broadcasted_iota(jnp.int32, (16, cells), 0) == 0, spot // LANES, spot % LANES
    ).astype(jnp.float32)
    high = flux.astype(jnp.bfloat16)
    low = (flux - high.astype(jnp.float32)).astype(jnp.bfloat16)
    parts = jnp.concatenate([high, low, spots.astype(jnp.bfloat16)], axis=0)
    lane_of = lax.broadcasted_iota(jnp.int32, (LANES, cells), 0)

    @pl.loop(0, blocks)
    def _(j):
        taken = (key - j * LANES == lane_of).astype(jnp.float32).astype(jnp.bfloat16)
        placed = lax.dot_general(
            parts, taken, (((1,), (1,)), ((), ())), preferred_element_type=jnp.float32
        )
        summed = placed[0:tr] + placed[tr : 2 * tr]
        slots[0, j] = summed[0:8]
        slots[1, j] = summed[8:16]
        slots[2, j] = placed[2 * tr : 2 * tr + 8]

    stacked = [slots[h].reshape(8 * blocks, LANES) for h in range(3)]
    laneb = lax.broadcasted_iota(jnp.int32, (8 * blocks, LANES), 1)
    for g in range(groups):
        turned = [
            pltpu.roll(s, (cap * (h - g)) % LANES, 1) if h != g else s
            for h, s in enumerate(stacked)
        ]
        packed = jnp.where(laneb < cap, turned[0], jnp.where(laneb < 2 * cap, turned[1], turned[2]))
        route_out[blocks * g : blocks * (g + 1)] = packed.reshape(blocks, 8, LANES)

    @pl.loop(1, count)
    def _(o):
        route_copy(lax.rem(me + o, count), me).start()

    route_in[place(me)] = route_out[place(me)]

    blow(lead // 2 + 1, lead)

    @pl.when(has_south)
    def _():
        mer_copy(1).wait_recv()

    @pl.when(has_north)
    def _():
        mer_copy(0).wait_recv()

    grid_row = lax.broadcasted_iota(jnp.int32, (3 * rows, LANES), 0) + (lat - 1) * rows
    northern = (grid_row < n_lat * rows - 1).astype(jnp.float32)

    @pl.loop(0, lev)
    def _(k):
        c = jnp.concatenate([mer_in[1, k], mer_ref[k], mer_in[0, k]], axis=0) * northern
        for m, weight in enumerate(cell_weights(c, pltpu.roll(c, 1, 0))):
            gm[k, m, 0 : 3 * rows] = weight

    route_all().wait_recv()
    route_all().wait_send()

    lists = [jnp.zeros((8 * blocks, LANES), jnp.float32)] * 3
    for g in range(groups):
        got = route_in[blocks * g : blocks * (g + 1)].reshape(8 * blocks, LANES)
        for h in range(3):
            turned = pltpu.roll(got, (cap * (g - h)) % LANES, 1) if g != h else got
            lists[h] = jnp.where(laneb // cap == g, turned, lists[h])
    entries = [
        jnp.concatenate([part[8 * j : 8 * (j + 1)] for j in range(blocks)], axis=1)
        for part in lists
    ]
    values = jnp.concatenate(entries[:2], axis=0)
    at_row, at_lane = entries[2][0:1], entries[2][1:2]
    wide = blocks * LANES
    onto = (
        lax.broadcasted_iota(jnp.int32, (LANES, wide), 0).astype(jnp.float32) == at_lane
    ).astype(jnp.float32)
    row_of = lax.broadcasted_iota(jnp.int32, (rows, wide), 0).astype(jnp.float32)
    spread = jnp.concatenate(
        [jnp.where(at_row == row_of, values[t : t + 1], 0.0) for t in range(tr)], axis=0
    )
    high = spread.astype(jnp.bfloat16)
    low = (spread - high.astype(jnp.float32)).astype(jnp.bfloat16)
    emitted = lax.dot_general(
        jnp.concatenate([high, low], axis=0),
        onto.astype(jnp.bfloat16),
        (((1,), (1,)), ((), ())),
        preferred_element_type=jnp.float32,
    )
    emitted = emitted[: rows * tr] + emitted[rows * tr :]

    surface = x_ref[:, 0].reshape(tr * rows, LANES) + emitted
    zb[0, own] = turned_by(straight, surface)
    lon_copy(2, 0).start()
    lon_copy(2, 1).start()

    def meridional(k):
        @pl.when(has_south)
        def _():
            lat_copy(k, 1).wait_recv()

        @pl.when(has_north)
        def _():
            lat_copy(k, 0).wait_recv()

        once = []
        for a in range(-3, rows + 3):
            new = 0.0
            for m in range(7):
                new = new + st[k, a + 3 + m] * gm[k, m, pl.ds(a + rows, tr, stride=0), :]
            once.append(new)
        for a in range(rows):
            new = 0.0
            for m in range(7):
                new = new + once[a + m] * gm[k, m, pl.ds(a + rows, tr, stride=0), :]
            fin[k, a] = new

    def mixed(levels, opening, closing):
        @pl.loop(0, rows)
        def _(a):
            part = [fin[j, a] for j in levels]
            for k in range(lev):
                total = 0.0 if opening else acc[a, k]
                for j, value in zip(levels, part):
                    total = total + value * mix_ref[a, k, j]
                acc[a, k] = total
            if closing:
                pltpu.make_async_copy(acc.at[a], out_ref.at[a], out_sem.at[a]).start()

    ordered = list(range(lead, lev)) + list(range(1, lead))
    share = len(ordered) // 3
    meet = lev - lead

    def some(i):
        levels = ordered[i * share : (i + 1) * share if i < 2 else None]
        first = 0

        if i == 0:

            @pl.loop(lead, lev)
            def _(k):
                meridional(k)

            first = meet

        @pl.loop(levels[first], levels[-1] + 1)
        def _(k):
            meridional(k)

        mixed(levels, i == 0, False)

    load(11).wait()
    some(0)
    lon_copy(2, 0).wait_recv()
    lon_copy(2, 1).wait_recv()
    zonal(0, 1)
    send_rows(0)
    some(1)
    some(2)
    meridional(0)
    mixed(range(1), False, True)

    @pl.loop(0, rows)
    def _(a):
        pltpu.make_async_copy(acc.at[a], out_ref.at[a], out_sem.at[a]).wait()

    for side in range(2):
        for part in range(3):
            lon_copy(part, side).wait_send()

    @pl.when(has_south)
    def _():
        mer_copy(0).wait_send()
        lat_all(0).wait_send()

    @pl.when(has_north)
    def _():
        mer_copy(1).wait_send()
        lat_all(1).wait_send()


def on_device(
    n_lat,
    n_lon,
    features,
    land_tile,
    land_spot,
    w_in,
    b_in,
    w_mid,
    b_mid,
    w_out,
    tracers,
    zonal_wind,
    meridional_wind,
    mixing,
):
    tr, lev, rows, cols = tracers.shape
    cells = features.shape[0]
    count = n_lat * n_lon
    cap = 2 * cells // count
    f32 = jnp.float32
    args = (
        features.T,
        land_tile.T,
        land_spot.reshape(1, -1),
        w_in,
        b_in.reshape(1, -1),
        w_mid,
        b_mid.reshape(1, -1),
        w_out.T,
        tracers,
        zonal_wind,
        meridional_wind,
        mixing,
    )
    out = pl.pallas_call(
        functools.partial(kernel, n_lat, n_lon, cap),
        out_shape=jax.ShapeDtypeStruct((rows, lev, tr, cols), f32),
        in_specs=[pl.BlockSpec(memory_space=pltpu.HBM)] * len(args),
        out_specs=pl.BlockSpec(memory_space=pltpu.HBM),
        scratch_shapes=[pltpu.VMEM(arg.shape, arg.dtype) for arg in args[:-1]]
        + [
            pltpu.SMEM(mixing.shape, f32),
            pltpu.SemaphoreType.DMA((len(args),)),
            pltpu.VMEM((lev + 1, cols + 32, tr * rows), f32),
            pltpu.VMEM((2, cols + 32, tr * rows), f32),
            pltpu.VMEM((2, cols, tr * rows), f32),
            pltpu.VMEM((7 * (cols + 16), 2 * lev * rows), jnp.bfloat16),
            pltpu.VMEM((7 * (cols + 16), 2 * tr * rows), f32),
            pltpu.VMEM((2, lev, rows, cols), f32),
            pltpu.VMEM((count, 8, cols), f32),
            pltpu.VMEM((count, 8, cols), f32),
            pltpu.VMEM((lev, 7, 3 * rows + tr, cols), f32),
            pltpu.VMEM((lev, rows + 2 * WIDE, tr, cols), f32),
            pltpu.VMEM((lev, rows, tr, cols), f32),
            pltpu.VMEM((rows, lev, tr, cols), f32),
            pltpu.VMEM((3, count * cap // cols, 8, cols), f32),
            pltpu.SemaphoreType.DMA((2, 3, 2)),
            pltpu.SemaphoreType.DMA((2, 2)),
            pltpu.SemaphoreType.DMA((1,)),
            pltpu.SemaphoreType.DMA((1,)),
            pltpu.SemaphoreType.DMA((2,)),
            pltpu.SemaphoreType.DMA((2, lev)),
            pltpu.SemaphoreType.DMA((rows,)),
        ],
        compiler_params=pltpu.CompilerParams(
            collective_id=0, has_side_effects=True, vmem_limit_bytes=60 * 1024 * 1024
        ),
    )(*args)
    return out.transpose(2, 1, 0, 3)


def solution(mesh):
    placed = (
        P(("lat", "lon"), None),
        P(("lat", "lon"), None),
        P(("lat", "lon")),
        P(),
        P(),
        P(),
        P(),
        P(),
        P(None, None, "lat", "lon"),
        P(None, "lat", "lon"),
        P(None, "lat", "lon"),
        P("lat", None, None),
    )
    return jax.shard_map(
        functools.partial(on_device, mesh.shape["lat"], mesh.shape["lon"]),
        mesh=mesh,
        in_specs=placed,
        out_specs=P(None, None, "lat", "lon"),
        check_vma=False,
    )
```
